32 devices in a mesh: dp: 4 (over y, core), seq: 8 (over z, x).
Axes of the slice: x: 2, y: 2, z: 4, core: 2. Of those that a mesh axis runs over, the one named last changes fastest.
Arguments:
- embedding: bfloat16 [8, 512, 1024], P('dp', 'seq'), may hold values from -6 to 6
- latent: bfloat16 [8, 512, 1024], P('dp', 'seq'), may hold values from -6 to 6
- segment_ids: int32 [8, 512], P('dp', 'seq'), may hold values from 0 to 5, as said below
- cotangent: bfloat16 [8, 512, 1024], P('dp', 'seq'), may hold values from -6 to 6
- weight_adapt: float32 [2048, 1024], P(('dp', 'seq')), may hold values from -0.125 to 0.125
- weight_attn: float32 [4, 1024, 1024], P(None, ('dp', 'seq')), may hold values from -0.1875 to 0.1875
- weight_gateup: float32 [2, 1024, 2816], P(None, ('dp', 'seq')), may hold values from -0.1875 to 0.1875
- weight_down: float32 [2816, 1024], P(('dp', 'seq')), may hold values from -0.109375 to 0.109375
- norm_gains: float32 [4, 1024], P(None, ('dp', 'seq')), may hold values from 0.5 to 1.5
- left_adapt: float32 [2048, 2048], P(('dp', 'seq')), may hold values from 0 to 4
- right_adapt: float32 [1024, 1024], P(('dp', 'seq')), may hold values from 0 to 4
- left_attn: float32 [4, 1024, 1024], P(None, ('dp', 'seq')), may hold values from 0 to 4
- right_attn: float32 [4, 1024, 1024], P(None, ('dp', 'seq')), may hold values from 0 to 4
- left_gateup: float32 [2, 1024, 1024], P(None, ('dp', 'seq')), may hold values from 0 to 4
- right_gateup: float32 [2, 2816, 2816], P(None, ('dp', 'seq')), may hold values from 0 to 4
- left_down: float32 [2816, 2816], P(('dp', 'seq')), may hold values from 0 to 4
- right_down: float32 [1024, 1024], P(('dp', 'seq')), may hold values from 0 to 4
- left_root_adapt: float32 [2048, 2048], P(('dp', 'seq')), may hold values from -1 to 2, as said below
- right_root_adapt: float32 [1024, 1024], P(('dp', 'seq')), may hold values from -1 to 2, as said below
- left_root_attn: float32 [4, 1024, 1024], P(None, ('dp', 'seq')), may hold values from -1 to 2, as said below
- right_root_attn: float32 [4, 1024, 1024], P(None, ('dp', 'seq')), may hold values from -1 to 2, as said below
- left_root_gateup: float32 [2, 1024, 1024], P(None, ('dp', 'seq')), may hold values from -1 to 2, as said below
- right_root_gateup: float32 [2, 2816, 2816], P(None, ('dp', 'seq')), may hold values from -1 to 2, as said below
- left_root_down: float32 [2816, 2816], P(('dp', 'seq')), may hold values from -1 to 2, as said below
- right_root_down: float32 [1024, 1024], P(('dp', 'seq')), may hold values from -1 to 2, as said below
- gain_moment: float32 [4, 1024], P(None, ('dp', 'seq')), may hold values from 1 to 4
Outputs:
- latent_out: bfloat16 [8, 512, 1024], P('dp', 'seq')
- grad_embedding: float32 [8, 512, 1024], P('dp', 'seq')
- grad_adapt: float32 [2048, 1024], P(('dp', 'seq'))
- grad_attn: float32 [4, 1024, 1024], P(None, ('dp', 'seq'))
- grad_gateup: float32 [2, 1024, 2816], P(None, ('dp', 'seq'))
- grad_down: float32 [2816, 1024], P(('dp', 'seq'))
- grad_gains: float32 [4, 1024], P(None, ('dp', 'seq'))
- new_left_adapt: float32 [2048, 2048], P(('dp', 'seq'))
- new_right_adapt: float32 [1024, 1024], P(('dp', 'seq'))
- new_left_attn: float32 [4, 1024, 1024], P(None, ('dp', 'seq'))
- new_right_attn: float32 [4, 1024, 1024], P(None, ('dp', 'seq'))
- new_left_gateup: float32 [2, 1024, 1024], P(None, ('dp', 'seq'))
- new_right_gateup: float32 [2, 2816, 2816], P(None, ('dp', 'seq'))
- new_left_down: float32 [2816, 2816], P(('dp', 'seq'))
- new_right_down: float32 [1024, 1024], P(('dp', 'seq'))
- new_adapt: float32 [2048, 1024], P(('dp', 'seq'))
- new_attn: float32 [4, 1024, 1024], P(None, ('dp', 'seq'))
- new_gateup: float32 [2, 1024, 2816], P(None, ('dp', 'seq'))
- new_down: float32 [2816, 1024], P(('dp', 'seq'))
- new_gain_moment: float32 [4, 1024], P(None, ('dp', 'seq'))
- new_norm_gains: float32 [4, 1024], P(None, ('dp', 'seq'))
The draws below stay inside these ranges and needn't reach their ends.
Inputs may be any that keep to these rules, and one draw needn't show every extreme that they name: `segment_ids`: along each sequence the ids never fall and start at 0. Among the 2 sequences of each index of dp, one is a single document. `left_root_adapt`: Symmetric. `right_root_adapt`: Symmetric. `left_root_attn`: Symmetric. `right_root_attn`: Symmetric. `left_root_gateup`: Symmetric. `right_root_gateup`: Symmetric. `left_root_down`: Symmetric. `right_root_down`: Symmetric.
All inputs are finite; a program needn't handle non-finite values.
Results may differ from the reference program's by a relative error of at most 0.028.
Values may be sent and summed in bfloat16 or wider, within the bound.
No kernel may reach another device: no remote copies, remote signals or barrier semaphores. Data moves between devices by JAX's collectives and lax.ppermute only.
A program may use at most 320 MiB of HBM per device.

```python
import math
import jax
import jax.numpy as jnp
from jax import lax

D = 1024
HEADS = 8
HEAD_DIM = 128
FF = 2816
SEQS = 2
DOCS = 6
FWD_ITERS = 1
LEN = 512
NSEQ = 8
N_DP = 4


def draw_segment_ids(key, part):
    key = jax.random.fold_in(key, 101)
    cut_key, pick_key = jax.random.split(key)
    cuts = jax.random.randint(cut_key, (NSEQ, DOCS - 1), 1, LEN)
    places = jnp.arange(LEN, dtype=jnp.int32)
    counted = jnp.sum((places[None, :, None] >= cuts[:, None, :]).astype(jnp.int32), axis=2)
    single = jax.random.randint(pick_key, (N_DP,), 0, SEQS)
    seq_index = jnp.arange(NSEQ, dtype=jnp.int32)
    whole_doc = seq_index % SEQS == single[seq_index // SEQS]
    return jnp.where(whole_doc[:, None], 0, counted).astype(jnp.int32)


def diagonal_stat(key, leading, order):
    uniform_draw = jax.random.uniform(key, leading + (order,), jnp.float32)
    diagonal = jnp.exp(uniform_draw * math.log(4.0))
    identity = jnp.eye(order, dtype=jnp.float32)
    return identity * diagonal[..., None, :]


def root_matrix(key, leading, order):
    diag_key, noise_key = jax.random.split(jax.random.fold_in(key, 7))
    uniform_draw = jax.random.uniform(diag_key, leading + (order,), jnp.float32)
    diagonal = 0.7 * jnp.exp(uniform_draw * math.log(2.0))
    noise = jax.random.normal(noise_key, leading + (order, order), jnp.float32)
    noise = (noise + jnp.swapaxes(noise, -1, -2)) * (0.25 / math.sqrt(2.0 * order))
    identity = jnp.eye(order, dtype=jnp.float32)
    return identity * diagonal[..., None, :] + (1.0 - identity) * noise


def draw_left_adapt(key, part):
    key = jax.random.fold_in(key, 11)
    return diagonal_stat(key, (), 2 * D)


def draw_right_adapt(key, part):
    key = jax.random.fold_in(key, 12)
    return diagonal_stat(key, (), D)


def draw_left_attn(key, part):
    key = jax.random.fold_in(key, 13)
    return diagonal_stat(key, (4,), D)


def draw_right_attn(key, part):
    key = jax.random.fold_in(key, 14)
    return diagonal_stat(key, (4,), D)


def draw_left_gateup(key, part):
    key = jax.random.fold_in(key, 15)
    return diagonal_stat(key, (2,), D)


def draw_right_gateup(key, part):
    key = jax.random.fold_in(key, 16)
    return diagonal_stat(key, (2,), FF)


def draw_left_down(key, part):
    key = jax.random.fold_in(key, 17)
    return diagonal_stat(key, (), FF)


def draw_right_down(key, part):
    key = jax.random.fold_in(key, 18)
    return diagonal_stat(key, (), D)


def draw_left_root_adapt(key, part):
    key = jax.random.fold_in(key, 21)
    return root_matrix(key, (), 2 * D)


def draw_right_root_adapt(key, part):
    key = jax.random.fold_in(key, 22)
    return root_matrix(key, (), D)


def draw_left_root_attn(key, part):
    key = jax.random.fold_in(key, 23)
    return root_matrix(key, (4,), D)


def draw_right_root_attn(key, part):
    key = jax.random.fold_in(key, 24)
    return root_matrix(key, (4,), D)


def draw_left_root_gateup(key, part):
    key = jax.random.fold_in(key, 25)
    return root_matrix(key, (2,), D)


def draw_right_root_gateup(key, part):
    key = jax.random.fold_in(key, 26)
    return root_matrix(key, (2,), FF)


def draw_left_root_down(key, part):
    key = jax.random.fold_in(key, 27)
    return root_matrix(key, (), FF)


def draw_right_root_down(key, part):
    key = jax.random.fold_in(key, 28)
    return root_matrix(key, (), D)


def level_of(key, shape, cuts, least, top_value):
    loudness, own = 1.0, jax.random.fold_in(key, 6)
    for position, blocks in cuts:
        heights = jnp.exp(jax.random.uniform(jax.random.fold_in(own, position), (blocks,), jnp.float32, least / len(cuts), top_value / len(cuts)))
        loudness = loudness * jnp.repeat(heights, shape[position] // blocks).reshape([-1 if axis == position else 1 for axis in range(len(shape))])
    return loudness


def normal_values(key, dims, spread, limit, cuts=(), held_as=jnp.bfloat16):
    drawn = jax.random.normal(key, dims, jnp.float32) * spread
    if len(cuts) > 0:
        drawn = level_of(key, dims, cuts, -0.22, 0.18) * drawn
    return jnp.clip(drawn, min=-limit, max=limit).astype(held_as)


def setup_inputs(seed: int = 0) -> dict:
    keys = jax.random.split(jax.random.key(seed), 27)
    return {
        "embedding": normal_values(keys[0], (NSEQ, LEN, D), 1.0, 6.0, ((0, 4), (1, 8))),
        "latent": normal_values(keys[1], (NSEQ, LEN, D), 1.0, 6.0, ((0, 4), (1, 8))),
        "segment_ids": draw_segment_ids(jax.random.fold_in(keys[26], 71), 0),
        "cotangent": normal_values(keys[3], (NSEQ, LEN, D), 1.0, 6.0, ((0, 4), (1, 8))),
        "weight_adapt": normal_values(keys[4], (2 * D, D), (2 * D) ** -0.5, 0.125, ((0, 32),), jnp.float32),
        "weight_attn": normal_values(keys[5], (4, D, D), D ** -0.5, 0.1875, ((1, 32),), jnp.float32),
        "weight_gateup": normal_values(keys[6], (2, D, FF), D ** -0.5, 0.1875, ((1, 32),), jnp.float32),
        "weight_down": normal_values(keys[7], (FF, D), FF ** -0.5, 0.109375, ((0, 32),), jnp.float32),
        "norm_gains": jnp.clip(1.0 + 0.1 * jax.random.normal(keys[8], (4, D), jnp.float32), 0.5, 1.5),
        "left_adapt": draw_left_adapt(jax.random.fold_in(keys[26], 71), 0),
        "right_adapt": draw_right_adapt(jax.random.fold_in(keys[26], 71), 0),
        "left_attn": draw_left_attn(jax.random.fold_in(keys[26], 71), 0),
        "right_attn": draw_right_attn(jax.random.fold_in(keys[26], 71), 0),
        "left_gateup": draw_left_gateup(jax.random.fold_in(keys[26], 71), 0),
        "right_gateup": draw_right_gateup(jax.random.fold_in(keys[26], 71), 0),
        "left_down": draw_left_down(jax.random.fold_in(keys[26], 71), 0),
        "right_down": draw_right_down(jax.random.fold_in(keys[26], 71), 0),
        "left_root_adapt": draw_left_root_adapt(jax.random.fold_in(keys[26], 71), 0),
        "right_root_adapt": draw_right_root_adapt(jax.random.fold_in(keys[26], 71), 0),
        "left_root_attn": draw_left_root_attn(jax.random.fold_in(keys[26], 71), 0),
        "right_root_attn": draw_right_root_attn(jax.random.fold_in(keys[26], 71), 0),
        "left_root_gateup": draw_left_root_gateup(jax.random.fold_in(keys[26], 71), 0),
        "right_root_gateup": draw_right_root_gateup(jax.random.fold_in(keys[26], 71), 0),
        "left_root_down": draw_left_root_down(jax.random.fold_in(keys[26], 71), 0),
        "right_root_down": draw_right_root_down(jax.random.fold_in(keys[26], 71), 0),
        "gain_moment": jnp.clip(jnp.exp(math.log(4.0) - 1.3862944 * jax.random.uniform(keys[25], (4, D), jnp.float32) ** level_of(keys[25], (4, D), ((1, 32),), -0.2, 0.2)), 1.0, 4.0),
    }


@jax.custom_vjp
def low(v):
    return lax.optimization_barrier(v.astype(jnp.bfloat16)).astype(jnp.float32)

@jax.custom_vjp
def low_back(v):
    return v

def low_keep(v):
    return (low(v), None)

def low_pass(kept, grad):
    return (grad,)

def back_keep(v):
    return (v, None)

def back_low(kept, grad):
    return (low(grad),)
low.defvjp(low_keep, low_pass)
low_back.defvjp(back_keep, back_low)
EPSILON = 1e-06
THETA = 50000.0
HIGHEST = lax.Precision.HIGHEST

def matmul(left_side, right_side):
    return jnp.dot(left_side, right_side, precision=HIGHEST, preferred_element_type=jnp.float32)

def rms_norm(values, gain_row):
    return values * lax.rsqrt(lax.optimization_barrier(jnp.mean(values * values, axis=-1, keepdims=True)) + EPSILON) * gain_row

def rotate(values, cosine, sine_table):
    half_dim = values.shape[-1] // 2
    first_half = values[..., :half_dim]
    second_half = values[..., half_dim:]
    return jnp.concatenate([first_half * cosine - second_half * sine_table, second_half * cosine + first_half * sine_table], axis=-1)

def rope_tables(segments):
    length = segments.shape[0]
    starts = lax.optimization_barrier(jnp.sum((segments[None, :] < segments[:, None]).astype(jnp.int32), axis=1))
    places = jnp.arange(length, dtype=jnp.int32) - starts
    half_dim = HEAD_DIM // 2
    frequency = THETA ** (-jnp.arange(half_dim, dtype=jnp.float32) / half_dim)
    angles = places.astype(jnp.float32)[:, None] * frequency[None, :]
    return (jnp.cos(angles)[:, None, :], jnp.sin(angles)[:, None, :])

def attention(queries, keys_all, values, segments):
    length = queries.shape[0]
    block_rows = min(512, length)
    key_index = jnp.arange(length, dtype=jnp.int32)
    scaling = 1.0 / math.sqrt(HEAD_DIM)

    def one_block(block_start):
        query_block = lax.dynamic_slice_in_dim(queries, block_start, block_rows, 0)
        segment_block = lax.dynamic_slice_in_dim(segments, block_start, block_rows, 0)
        query_index = block_start + jnp.arange(block_rows, dtype=jnp.int32)
        scores = low_back(jnp.einsum('qhd,khd->hqk', query_block, keys_all, precision=HIGHEST) * scaling)
        allowed = (key_index[None, :] <= query_index[:, None]) & (segments[None, :] == segment_block[:, None])
        scores = jnp.where(allowed[None], scores, -1e+30)
        row_top = lax.optimization_barrier(jnp.max(scores, axis=-1, keepdims=True))
        exponent = jnp.exp(scores - row_top)
        soft_weights = low(exponent / lax.optimization_barrier(jnp.sum(exponent, axis=-1, keepdims=True)))
        mixed_heads = jnp.einsum('hqk,khd->qhd', soft_weights, values, precision=HIGHEST)
        return mixed_heads.reshape(block_rows, -1)
    starts = jnp.arange(length // block_rows, dtype=jnp.int32) * block_rows
    blocks = lax.map(jax.checkpoint(one_block), starts)
    return low(low_back(blocks.reshape(length, -1)))

def sequence_layer(params, latent_row, embed_row, segments):
    adapt_low, attn_low, gateup_low, down_low, gain_low = params
    length = latent_row.shape[0]
    joined = jnp.concatenate([low(latent_row), embed_row], axis=-1)
    start_sum = low_back(matmul(joined, adapt_low))
    normed_one = low(rms_norm(start_sum, gain_low[0]))
    cosine, sine_table = rope_tables(segments)
    head_shape = (length, HEADS, HEAD_DIM)
    queries = low(rotate(low_back(matmul(normed_one, attn_low[0])).reshape(head_shape), cosine, sine_table))
    keys_all = low(rotate(low_back(matmul(normed_one, attn_low[1])).reshape(head_shape), cosine, sine_table))
    values = low(low_back(matmul(normed_one, attn_low[2]))).reshape(head_shape)
    mixed_heads = attention(queries, keys_all, values, segments)
    branch = low_back(matmul(mixed_heads, attn_low[3]))
    middle = start_sum + rms_norm(branch, gain_low[1])
    normed_three = low(rms_norm(middle, gain_low[2]))
    gate_value = low_back(matmul(normed_three, gateup_low[0]))
    upward = low_back(matmul(normed_three, gateup_low[1]))
    hidden = low(jax.nn.silu(gate_value) * upward)
    feed_out = low_back(matmul(hidden, down_low))
    return middle + rms_norm(feed_out, gain_low[3])

def layer_all(params, latent_all, embed_all, segment_all):

    def per_sequence(carry_value, seq_row):
        return (carry_value, jax.checkpoint(sequence_layer)(params, seq_row[0], seq_row[1], seq_row[2]))
    unused_carry, outputs = lax.scan(per_sequence, jnp.zeros((), jnp.float32), (latent_all, embed_all, segment_all))
    return outputs

def shampoo(weight, gradient, left_stat, right_stat, left_root, right_root):
    row_count, col_count = gradient.shape
    new_left = 0.5 * left_stat + 0.5 * matmul(gradient, gradient.T) / col_count
    new_right = 0.5 * right_stat + 0.5 * matmul(gradient.T, gradient) / row_count
    update = matmul(matmul(left_root, gradient), right_root)
    return (new_left, new_right, weight - update / math.sqrt(row_count))

def reference(embedding, latent, segment_ids, cotangent, weight_adapt, weight_attn, weight_gateup, weight_down, norm_gains, left_adapt, right_adapt, left_attn, right_attn, left_gateup, right_gateup, left_down, right_down, left_root_adapt, right_root_adapt, left_root_attn, right_root_attn, left_root_gateup, right_root_gateup, left_root_down, right_root_down, gain_moment):
    embed_full = embedding.astype(jnp.float32)
    weights = (weight_adapt, weight_attn, weight_gateup, weight_down, norm_gains)
    latent_state = latent.astype(jnp.float32)
    for repeat in range(FWD_ITERS):
        latent_state = layer_all(tuple((low(member) for member in weights)), latent_state, embed_full, segment_ids)

    def whole_layer(params, embed_values):
        return layer_all(tuple((low(member) for member in params)), latent_state, embed_values, segment_ids)
    final_state, pullback = jax.vjp(whole_layer, weights, embed_full)
    weight_grads, grad_embedding = pullback(cotangent.astype(jnp.float32))
    factor = 1.0 / math.sqrt(NSEQ * LEN)
    grad_adapt = weight_grads[0] * factor
    grad_attn = weight_grads[1] * factor
    grad_gateup = weight_grads[2] * factor
    grad_down = weight_grads[3] * factor
    grad_gains = weight_grads[4] * factor
    new_left_adapt, new_right_adapt, new_adapt = shampoo(weight_adapt, grad_adapt, left_adapt, right_adapt, left_root_adapt, right_root_adapt)
    attn_parts = [shampoo(weight_attn[index], grad_attn[index], left_attn[index], right_attn[index], left_root_attn[index], right_root_attn[index]) for index in range(4)]
    gateup_parts = [shampoo(weight_gateup[index], grad_gateup[index], left_gateup[index], right_gateup[index], left_root_gateup[index], right_root_gateup[index]) for index in range(2)]
    new_left_down, new_right_down, new_down = shampoo(weight_down, grad_down, left_down, right_down, left_root_down, right_root_down)
    new_left_attn = jnp.stack([member[0] for member in attn_parts])
    new_right_attn = jnp.stack([member[1] for member in attn_parts])
    new_attn = jnp.stack([member[2] for member in attn_parts])
    new_left_gateup = jnp.stack([member[0] for member in gateup_parts])
    new_right_gateup = jnp.stack([member[1] for member in gateup_parts])
    new_gateup = jnp.stack([member[2] for member in gateup_parts])
    new_gain_moment = 0.5 * gain_moment + 0.5 * grad_gains * grad_gains
    new_norm_gains = norm_gains - 0.5 * grad_gains / (jnp.sqrt(new_gain_moment) + 1e-08)
    return (final_state.astype(jnp.bfloat16), grad_embedding, grad_adapt, grad_attn, grad_gateup, grad_down, grad_gains, new_left_adapt, new_right_adapt, new_left_attn, new_right_attn, new_left_gateup, new_right_gateup, new_left_down, new_right_down, new_adapt, new_attn, new_gateup, new_down, new_gain_moment, new_norm_gains)
```

```python
import math

import jax
import jax.numpy as jnp
from jax import lax
from jax.sharding import PartitionSpec as P

HEADS = 8
HEAD_DIM = 128
EPSILON = 1e-06
THETA = 50000.0
AXES = ("dp", "seq")
BF16 = jnp.bfloat16
F32 = jnp.float32


def product(left_side, right_side):
    return jnp.dot(left_side, right_side, preferred_element_type=F32)


def across(left_side, right_side):
    return lax.dot_general(
        left_side, right_side, (((0,), (0,)), ((), ())), preferred_element_type=F32
    )


def against(left_side, right_side):
    return lax.dot_general(
        left_side, right_side, (((1,), (1,)), ((), ())), preferred_element_type=F32
    )


def norm_scale(values):
    return lax.rsqrt(jnp.mean(values * values, axis=-1, keepdims=True) + EPSILON)


def norm_back(values, scaling, gain_row, gradient):
    unit_rows = values * scaling
    weighted = gradient * gain_row
    moved = scaling * (
        weighted - unit_rows * jnp.mean(unit_rows * weighted, axis=-1, keepdims=True)
    )
    return (moved, jnp.sum(gradient * unit_rows, axis=0))


def rotate(values, cosine, sine_table):
    half_dim = values.shape[-1] // 2
    first_half = values[..., :half_dim]
    second_half = values[..., half_dim:]
    return jnp.concatenate(
        [
            first_half * cosine - second_half * sine_table,
            second_half * cosine + first_half * sine_table,
        ],
        axis=-1,
    )


def silu_grad(values):
    sigmoid_value = jax.nn.sigmoid(values)
    return sigmoid_value * (1.0 + values * (1.0 - sigmoid_value))


class Links:
    def __init__(self, n_dp, n_seq):
        self.n_dp, self.n_seq = n_dp, n_seq
        self.sizes = (n_dp // 2, 2, n_seq // 2, 2)
        self.count = n_dp * n_seq
        dp, seq = lax.axis_index("dp"), lax.axis_index("seq")
        self.place = (dp // 2, dp % 2, seq // 2, seq % 2)
        self.index = dp * n_seq + seq
        self.seq_index = seq

    def digits(self, index):
        out = []
        for size in reversed(self.sizes):
            out.append(index % size)
            index //= size
        return out[::-1]

    def number(self, digits):
        index = 0
        for digit, size in zip(digits, self.sizes):
            index = index * size + digit
        return index

    def move(self, values, digit, step):
        pairs = []
        for source in range(self.count):
            target = self.digits(source)
            target[digit] = (target[digit] + step) % self.sizes[digit]
            pairs.append((source, self.number(target)))
        return lax.ppermute(values, AXES, pairs)

    def total(self, values, digits):
        for digit in digits:
            size = self.sizes[digit]
            bit = 1
            while bit < size:
                pairs = []
                for source in range(self.count):
                    target = self.digits(source)
                    target[digit] ^= bit
                    pairs.append((source, self.number(target)))
                values = values + lax.ppermute(values, AXES, pairs)
                bit *= 2
        return values

    def _put(self, whole, part, axis, where, column):
        starts = [0] * whole.ndim
        starts[axis] = where
        starts[-1] = column
        return lax.dynamic_update_slice(whole, jnp.expand_dims(part, axis), tuple(starts))

    def gather(self, shard):
        rows, columns = shard.shape
        half = columns // 2
        whole = jnp.zeros(self.sizes + (rows, columns), shard.dtype)
        for start, order in ((0, (2, 3, 0)), (half, (2, 0, 3))):
            part = shard[:, start : start + half]
            known = []
            for digit in order:
                axis = sum(1 for other in known if other < digit)
                size = self.sizes[digit]
                shape = part.shape[:axis] + (size,) + part.shape[axis:]
                wider = jnp.zeros(shape, part.dtype)
                wider = self._put(wider, part, axis, self.place[digit], 0)
                for step in range(1, size):
                    came = self.move(part, digit, step)
                    wider = self._put(wider, came, axis, (self.place[digit] - step) % size, 0)
                part = wider
                known.append(digit)
            came = self.move(part, 1, 1)
            whole = self._put(whole, part, 1, self.place[1], start)
            whole = self._put(whole, came, 1, 1 - self.place[1], start)
        return whole.reshape(self.count * rows, columns)

    def reduce(self, left_side, right_side):
        tokens, height = left_side.shape
        columns = right_side.shape[1]
        rows = height // self.count
        first, second, third, fourth = self.sizes
        sides = left_side.reshape(tokens, first, 2, third * fourth * rows)
        shape = (first, third, fourth, rows, columns)

        def term(which):
            side = lax.dynamic_index_in_dim(sides, which, 2, False).reshape(tokens, -1)
            return across(side, right_side)

        away = term(1 - self.place[1]).astype(BF16)
        came = self.move(away, 1, 1)
        total = (term(self.place[1]) + came.astype(F32)).astype(BF16).reshape(shape)
        half = columns // 2
        parts = []
        for start, order in ((0, (0, 3, 2)), (half, (3, 0, 2))):
            part = total[..., start : start + half]
            left = [0, 2, 3]
            for digit in order:
                axis, size = left.index(digit), self.sizes[digit]
                place = self.place[digit]
                summed = lax.dynamic_index_in_dim(part, place, axis, False).astype(F32)
                for step in range(1, size):
                    away = lax.dynamic_index_in_dim(part, (place + step) % size, axis, False)
                    summed = summed + self.move(away, digit, step).astype(F32)
                left.remove(digit)
                part = summed.astype(BF16) if left else summed
            parts.append(part)
        return jnp.concatenate(parts, axis=1)


def body(
    embedding,
    latent,
    segment_ids,
    cotangent,
    weight_adapt,
    weight_attn,
    weight_gateup,
    weight_down,
    norm_gains,
    left_adapt,
    right_adapt,
    left_attn,
    right_attn,
    left_gateup,
    right_gateup,
    left_down,
    right_down,
    left_root_adapt,
    right_root_adapt,
    left_root_attn,
    right_root_attn,
    left_root_gateup,
    right_root_gateup,
    left_root_down,
    right_root_down,
    gain_moment,
):
    n_dp, n_seq = lax.axis_size("dp"), lax.axis_size("seq")
    links = Links(n_dp, n_seq)
    seq_count, group_len, width = embedding.shape
    tokens = seq_count * group_len
    length = group_len * n_seq
    hidden_width = weight_gateup.shape[2]
    by_heads = HEADS % n_seq == 0

    adapt_full = links.gather(weight_adapt.astype(BF16))
    attn_rows = weight_attn.astype(BF16)
    qkv_full = links.gather(jnp.concatenate([attn_rows[0], attn_rows[1], attn_rows[2]], axis=1))
    out_full = links.gather(attn_rows[3])
    gateup_rows = weight_gateup.astype(BF16)
    gateup_full = links.gather(jnp.concatenate([gateup_rows[0], gateup_rows[1]], axis=1))
    down_full = links.gather(weight_down.astype(BF16))

    gain_share = norm_gains.shape[1]
    gain_values = lax.dynamic_update_slice(
        jnp.zeros((4, width), F32),
        norm_gains.astype(BF16).astype(F32),
        (0, links.index * gain_share),
    )
    gain_values = links.total(gain_values, (0, 1, 2, 3))
    segment_whole = lax.dynamic_update_slice(
        jnp.zeros((seq_count, length), jnp.int32), segment_ids, (0, links.seq_index * group_len)
    )
    segment_whole = links.total(segment_whole, (2, 3))

    all_places = jnp.arange(length, dtype=jnp.int32)
    doc_starts = jnp.sum(
        (segment_whole[:, None, :] < segment_whole[:, :, None]).astype(jnp.int32), axis=2
    )
    places = all_places[None, :] - doc_starts
    half_dim = HEAD_DIM // 2
    frequency = THETA ** (-jnp.arange(half_dim, dtype=F32) / half_dim)
    angles = places.astype(F32)[..., None] * frequency
    cosine_all, sine_all = jnp.cos(angles), jnp.sin(angles)
    own_start = links.seq_index * group_len
    cosine = lax.dynamic_slice_in_dim(cosine_all, own_start, group_len, 1)
    sine_table = lax.dynamic_slice_in_dim(sine_all, own_start, group_len, 1)
    if by_heads:
        query_places, segment_query = all_places, segment_whole
        cosine_back, sine_back = cosine_all[:, None], sine_all[:, None]
    else:
        query_places, segment_query = own_start + jnp.arange(group_len), segment_ids
        cosine_back, sine_back = cosine[:, None], sine_table[:, None]
    allowed = (all_places[None, None, :] <= query_places[None, :, None]) & (
        segment_whole[:, None, :] == segment_query[:, :, None]
    )

    def to_heads(values):
        parts = values.shape[2]
        values = values.transpose(3, 2, 0, 1, 4)
        came = lax.all_to_all(values, "seq", 0, 0, tiled=True)
        came = came.reshape(n_seq, HEADS // n_seq, parts, seq_count, group_len, HEAD_DIM)
        came = came.transpose(2, 3, 1, 0, 4, 5)
        return came.reshape(parts, seq_count, HEADS // n_seq, length, HEAD_DIM)

    def to_tokens(values):
        parts = values.shape[0]
        own = HEADS // n_seq
        values = values.reshape(parts, seq_count, own, n_seq, group_len, HEAD_DIM)
        values = values.transpose(3, 2, 0, 1, 4, 5)
        came = lax.all_to_all(values, "seq", 0, 0, tiled=True)
        came = came.reshape(HEADS, parts, seq_count, group_len, HEAD_DIM)
        return came.transpose(1, 2, 3, 0, 4)

    scaling = 1.0 / math.sqrt(HEAD_DIM)

    def attention(queries, keys, values):
        if by_heads:
            queries, keys, values = to_heads(jnp.stack([queries, keys, values], axis=2))
        else:
            queries = queries.transpose(0, 2, 1, 3)
            keys, values = (
                lax.all_gather(item, "seq", axis=1, tiled=True).transpose(0, 2, 1, 3)
                for item in (keys, values)
            )
        scores = jnp.einsum("shqd,shkd->shqk", queries, keys, preferred_element_type=F32)
        scores = jnp.where(allowed[:, None], scores * scaling, -1e30)
        exponent = jnp.exp(scores - jnp.max(scores, axis=-1, keepdims=True))
        soft_full = exponent / jnp.sum(exponent, axis=-1, keepdims=True)
        mixed = jnp.einsum(
            "shqk,shkd->shqd", soft_full.astype(BF16), values, preferred_element_type=F32
        ).astype(BF16)
        if by_heads:
            mixed = to_tokens(mixed[None])[0]
        else:
            mixed = mixed.transpose(0, 2, 1, 3)
        return mixed.reshape(tokens, width), (queries, keys, values, soft_full)

    def attention_back(mixed_grad, saved):
        queries, keys, values, soft_full = saved
        mixed_grad = mixed_grad.reshape(seq_count, group_len, HEADS, HEAD_DIM)
        if by_heads:
            mixed_grad = to_heads(mixed_grad[:, :, None])[0]
        else:
            mixed_grad = mixed_grad.transpose(0, 2, 1, 3)
        soft_grad = jnp.einsum("shqd,shkd->shqk", mixed_grad, values, preferred_element_type=F32)
        inner_sum = jnp.sum(soft_full * soft_grad, axis=-1, keepdims=True)
        score_grad = (soft_full * (soft_grad - inner_sum)).astype(BF16)
        query_grad = (
            jnp.einsum("shqk,shkd->shqd", score_grad, keys, preferred_element_type=F32) * scaling
        )
        key_grad = (
            jnp.einsum("shqk,shqd->shkd", score_grad, queries, preferred_element_type=F32)
            * scaling
        )
        value_grad = jnp.einsum(
            "shqk,shqd->shkd", soft_full.astype(BF16), mixed_grad, preferred_element_type=F32
        )
        if by_heads:
            query_grad = rotate(query_grad, cosine_back, -sine_back).astype(BF16)
            key_grad = rotate(key_grad, cosine_back, -sine_back).astype(BF16)
            value_grad = value_grad.astype(BF16)
            grads = to_tokens(jnp.stack([query_grad, key_grad, value_grad]))
        else:
            key_grad, value_grad = (
                lax.psum_scatter(
                    item.astype(BF16), "seq", scatter_dimension=2, tiled=True
                ).astype(F32)
                for item in (key_grad, value_grad)
            )
            query_grad = rotate(query_grad, cosine_back, -sine_back).astype(BF16)
            key_grad = rotate(key_grad, cosine_back, -sine_back).astype(BF16)
            grads = jnp.stack([query_grad, key_grad, value_grad.astype(BF16)])
            grads = grads.transpose(0, 1, 3, 2, 4)
        return grads.reshape(3, tokens, width)

    embed_flat = embedding.reshape(tokens, width)
    embed_part = product(embed_flat, adapt_full[width:])

    def forward(latent_low):
        start_sum = product(latent_low, adapt_full[:width]) + embed_part
        scale_one = norm_scale(start_sum)
        normed_one = (start_sum * scale_one * gain_values[0]).astype(BF16)
        qkv = product(normed_one, qkv_full).reshape(seq_count, group_len, 3, HEADS, HEAD_DIM)
        turn_cos, turn_sin = cosine[:, :, None, :], sine_table[:, :, None, :]
        queries = rotate(qkv[:, :, 0], turn_cos, turn_sin).astype(BF16)
        keys = rotate(qkv[:, :, 1], turn_cos, turn_sin).astype(BF16)
        mixed_heads, attended = attention(queries, keys, qkv[:, :, 2].astype(BF16))
        branch = product(mixed_heads, out_full)
        scale_two = norm_scale(branch)
        middle = start_sum + branch * scale_two * gain_values[1]
        scale_three = norm_scale(middle)
        normed_three = (middle * scale_three * gain_values[2]).astype(BF16)
        both = product(normed_three, gateup_full)
        gate_value, upward = both[:, :hidden_width], both[:, hidden_width:]
        hidden = (jax.nn.silu(gate_value) * upward).astype(BF16)
        feed_out = product(hidden, down_full)
        scale_four = norm_scale(feed_out)
        result = middle + feed_out * scale_four * gain_values[3]
        saved_values = (
            start_sum,
            scale_one,
            normed_one,
            attended,
            mixed_heads,
            branch,
            scale_two,
            middle,
            scale_three,
            normed_three,
            gate_value,
            upward,
            hidden,
            feed_out,
            scale_four,
        )
        return (result, saved_values)

    latent_low = latent.reshape(tokens, width)
    latent_state, unused_saved = forward(latent_low)
    latent_low = latent_state.astype(BF16)
    final_state, saved_values = forward(latent_low)
    (
        start_sum,
        scale_one,
        normed_one,
        attended,
        mixed_heads,
        branch,
        scale_two,
        middle,
        scale_three,
        normed_three,
        gate_value,
        upward,
        hidden,
        feed_out,
        scale_four,
    ) = saved_values
    factor = 1.0 / math.sqrt(seq_count * n_dp * length)
    incoming = cotangent.astype(F32).reshape(tokens, width)
    feed_grad, gain_four = norm_back(feed_out, scale_four, gain_values[3], incoming)
    feed_grad = feed_grad.astype(BF16)
    reduced_down = links.reduce(hidden, feed_grad) * factor
    full_down = links.gather(reduced_down.astype(BF16))
    hidden_grad = against(feed_grad, down_full)
    gate_grad = (hidden_grad * upward * silu_grad(gate_value)).astype(BF16)
    up_grad = (hidden_grad * jax.nn.silu(gate_value)).astype(BF16)
    both_grad = jnp.concatenate([gate_grad, up_grad], axis=1)
    reduced_both = links.reduce(normed_three, both_grad) * factor
    full_both = links.gather(reduced_both.astype(BF16))
    normed_three_grad = against(both_grad, gateup_full)
    middle_grad, gain_three = norm_back(middle, scale_three, gain_values[2], normed_three_grad)
    middle_grad = middle_grad + incoming
    branch_grad, gain_two = norm_back(branch, scale_two, gain_values[1], middle_grad)
    branch_grad = branch_grad.astype(BF16)
    reduced_out = links.reduce(mixed_heads, branch_grad) * factor
    full_out = links.gather(reduced_out.astype(BF16))
    mixed_grad = against(branch_grad, out_full).astype(BF16)
    query_pre, key_pre, value_pre = attention_back(mixed_grad, attended)
    qkv_grad = jnp.concatenate([query_pre, key_pre, value_pre], axis=1)
    reduced_qkv = links.reduce(normed_one, qkv_grad) * factor
    full_qkv = links.gather(reduced_qkv.astype(BF16))
    normed_one_grad = against(qkv_grad, qkv_full)
    start_grad, gain_one = norm_back(start_sum, scale_one, gain_values[0], normed_one_grad)
    start_grad = (start_grad + middle_grad).astype(BF16)
    joined = jnp.concatenate([latent_low, embed_flat], axis=1)
    reduced_adapt = links.reduce(joined, start_grad) * factor
    full_adapt = links.gather(reduced_adapt.astype(BF16))
    grad_embedding = against(start_grad, adapt_full[width:]).reshape(
        seq_count, group_len, width
    )
    gain_sums = links.total(jnp.stack([gain_one, gain_two, gain_three, gain_four]), (0, 1, 2, 3))
    reduced_gains = (
        lax.dynamic_slice_in_dim(gain_sums, links.index * gain_share, gain_share, 1) * factor
    )

    root_stack = jnp.concatenate(
        [
            right_root_adapt.astype(BF16)[:, None],
            right_root_attn.astype(BF16).transpose(1, 0, 2),
            right_root_down.astype(BF16)[:, None],
            left_root_gateup.astype(BF16).transpose(1, 0, 2),
        ],
        axis=1,
    )
    share = root_stack.shape[0]
    roots = lax.all_gather(root_stack.reshape(share, 8 * width), AXES, axis=0, tiled=True)

    def statistics(shard, whole, left_stat, right_stat, left_root):
        rows, columns = whole.shape
        new_left = 0.5 * left_stat + (0.5 / columns) * against(shard.astype(BF16), whole)
        count = right_stat.shape[0]
        own = lax.dynamic_slice_in_dim(whole, links.index * count, count, 1).T
        if left_root is None:
            return (new_left, 0.5 * right_stat + (0.5 / rows) * product(own, whole), None)
        own_count = left_root.shape[0]
        both = product(jnp.concatenate([left_root.astype(BF16), own], axis=0), whole)
        return (new_left, 0.5 * right_stat + (0.5 / rows) * both[own_count:], both[:own_count])

    def step(part, which, rows):
        root = roots[:, which * width : (which + 1) * width]
        return product(part.astype(BF16), root) * (1.0 / math.sqrt(rows))

    whole_gates = [full_both[:, :hidden_width], full_both[:, hidden_width:]]
    gate_shards = [reduced_both[:, :hidden_width], reduced_both[:, hidden_width:]]
    gateup_parts = [
        statistics(gate_shards[i], whole_gates[i], left_gateup[i], right_gateup[i], None)
        for i in range(2)
    ]
    step_columns = []
    for i in range(2):
        turned = against(whole_gates[i], right_root_gateup[i].astype(BF16)).astype(BF16)
        root = roots[:, (6 + i) * width : (7 + i) * width]
        step_columns.append(product(root, turned).astype(BF16))
    step_columns = jnp.stack(step_columns)
    ff_share = step_columns.shape[2]
    row_share = width // links.count
    step_columns = step_columns.reshape(2, links.count, row_share, ff_share).transpose(1, 0, 2, 3)
    step_rows = lax.all_to_all(step_columns, AXES, 0, 0, tiled=True)
    step_gateup = step_rows.transpose(1, 2, 0, 3).reshape(2, row_share, hidden_width)
    new_gateup = weight_gateup - step_gateup.astype(F32) * (1.0 / math.sqrt(width))

    new_left_down, new_right_down, down_part = statistics(
        reduced_down, full_down, left_down, right_down, left_root_down
    )
    new_down = weight_down - step(down_part, 5, hidden_width)
    attn_shards = [reduced_qkv[:, i * width : (i + 1) * width] for i in range(3)] + [reduced_out]
    attn_wholes = [full_qkv[:, i * width : (i + 1) * width] for i in range(3)] + [full_out]
    attn_parts = [
        statistics(attn_shards[i], attn_wholes[i], left_attn[i], right_attn[i], left_root_attn[i])
        for i in range(4)
    ]
    new_attn = weight_attn - jnp.stack([step(attn_parts[i][2], 1 + i, width) for i in range(4)])
    new_left_adapt, new_right_adapt, adapt_part = statistics(
        reduced_adapt, full_adapt, left_adapt, right_adapt, left_root_adapt
    )
    new_adapt = weight_adapt - step(adapt_part, 0, 2 * width)
    new_gain_moment = 0.5 * gain_moment + 0.5 * reduced_gains * reduced_gains
    new_norm_gains = norm_gains - 0.5 * reduced_gains / (jnp.sqrt(new_gain_moment) + 1e-08)
    latent_out = final_state.reshape(seq_count, group_len, width).astype(BF16)
    return (
        latent_out,
        grad_embedding,
        reduced_adapt,
        jnp.stack(attn_shards),
        jnp.stack(gate_shards),
        reduced_down,
        reduced_gains,
        new_left_adapt,
        new_right_adapt,
        jnp.stack([member[0] for member in attn_parts]),
        jnp.stack([member[1] for member in attn_parts]),
        jnp.stack([member[0] for member in gateup_parts]),
        jnp.stack([member[1] for member in gateup_parts]),
        new_left_down,
        new_right_down,
        new_adapt,
        new_attn,
        new_gateup,
        new_down,
        new_gain_moment,
        new_norm_gains,
    )

def solution(mesh):
    return jax.shard_map(
        body,
        mesh=mesh,
        in_specs=(
            P("dp", "seq", None),
            P("dp", "seq", None),
            P("dp", "seq"),
            P("dp", "seq", None),
            P(("dp", "seq"), None),
            P(None, ("dp", "seq"), None),
            P(None, ("dp", "seq"), None),
            P(("dp", "seq"), None),
            P(None, ("dp", "seq")),
            P(("dp", "seq"), None),
            P(("dp", "seq"), None),
            P(None, ("dp", "seq"), None),
            P(None, ("dp", "seq"), None),
            P(None, ("dp", "seq"), None),
            P(None, ("dp", "seq"), None),
            P(("dp", "seq"), None),
            P(("dp", "seq"), None),
            P(("dp", "seq"), None),
            P(("dp", "seq"), None),
            P(None, ("dp", "seq"), None),
            P(None, ("dp", "seq"), None),
            P(None, ("dp", "seq"), None),
            P(None, ("dp", "seq"), None),
            P(("dp", "seq"), None),
            P(("dp", "seq"), None),
            P(None, ("dp", "seq")),
        ),
        out_specs=(
            P("dp", "seq", None),
            P("dp", "seq", None),
            P(("dp", "seq"), None),
            P(None, ("dp", "seq"), None),
            P(None, ("dp", "seq"), None),
            P(("dp", "seq"), None),
            P(None, ("dp", "seq")),
            P(("dp", "seq"), None),
            P(("dp", "seq"), None),
            P(None, ("dp", "seq"), None),
            P(None, ("dp", "seq"), None),
            P(None, ("dp", "seq"), None),
            P(None, ("dp", "seq"), None),
            P(("dp", "seq"), None),
            P(("dp", "seq"), None),
            P(("dp", "seq"), None),
            P(None, ("dp", "seq"), None),
            P(None, ("dp", "seq"), None),
            P(("dp", "seq"), None),
            P(None, ("dp", "seq")),
            P(None, ("dp", "seq")),
        ),
        check_vma=False,
    )
```

```python
import math

import jax
import jax.numpy as jnp
from jax import lax
from jax.experimental import pallas as pl
from jax.experimental.pallas import tpu as pltpu
from jax.sharding import PartitionSpec as P

HEADS = 8
HEAD_DIM = 128
EPSILON = 1e-06
THETA = 50000.0
AXES = ("dp", "seq")
BF16 = jnp.bfloat16
F32 = jnp.float32


def product(left_side, right_side):
    return jnp.dot(left_side, right_side, preferred_element_type=F32)


def across(left_side, right_side):
    return lax.dot_general(
        left_side, right_side, (((0,), (0,)), ((), ())), preferred_element_type=F32
    )


def against(left_side, right_side):
    return lax.dot_general(
        left_side, right_side, (((1,), (1,)), ((), ())), preferred_element_type=F32
    )


def norm_scale(values):
    return lax.rsqrt(jnp.mean(values * values, axis=-1, keepdims=True) + EPSILON)


def norm_back(values, scaling, gain_row, gradient):
    unit_rows = values * scaling
    weighted = gradient * gain_row
    moved = scaling * (
        weighted - unit_rows * jnp.mean(unit_rows * weighted, axis=-1, keepdims=True)
    )
    return (moved, jnp.sum(gradient * unit_rows, axis=0))


def rotate(values, cosine, sine_table):
    half_dim = values.shape[-1] // 2
    first_half = values[..., :half_dim]
    second_half = values[..., half_dim:]
    return jnp.concatenate(
        [
            first_half * cosine - second_half * sine_table,
            second_half * cosine + first_half * sine_table,
        ],
        axis=-1,
    )


def silu_grad(values):
    sigmoid_value = jax.nn.sigmoid(values)
    return sigmoid_value * (1.0 + values * (1.0 - sigmoid_value))


def tie(*values):
    return lax.optimization_barrier(values)


def tick(works, *values):
    flat = [part for work in works for part in work.parts]
    tied = list(lax.optimization_barrier(tuple(flat) + values))
    for work in works:
        count = len(work.parts)
        work.parts, tied = tied[:count], tied[count:]
    return tied


class Links:
    def __init__(self, n_dp, n_seq):
        self.count = n_dp * n_seq
        self.bits = (self.count - 1).bit_length()
        self.core = (n_dp - 1).bit_length() - 1
        self.last = self.bits - 1
        self.upper = list(range(self.core))
        self.inner = list(range(self.core + 1, self.last))
        self.index = lax.axis_index("dp") * n_seq + lax.axis_index("seq")
        self.seq_index = lax.axis_index("seq")
        self.pairs = [
            [(i, i ^ (1 << (self.bits - 1 - bit))) for i in range(self.count)]
            for bit in range(self.bits)
        ]
        self.steps = len(self.upper) + 1

    def own(self, bit):
        return (self.index >> (self.bits - 1 - bit)) & 1

    def swap(self, values, bit):
        return lax.ppermute(values, AXES, self.pairs[bit])


class Gathering:
    def __init__(self, links, shards):
        self.links = links
        self.heights = [shard.shape[0] for shard in shards]
        self.rows = sum(self.heights)
        shard = shards[0] if len(shards) == 1 else jnp.concatenate(shards, axis=0)
        self.parts = [shard]
        self.known = [[]]

    def widen(self, i, bit):
        links, part, known = self.links, self.parts[i], self.known[i]
        came = links.swap(part, bit)
        columns = part.shape[1]
        before = 1 << sum(1 for other in known if other < bit)
        mine = part.reshape(before, 1, -1, columns)
        both = jnp.zeros((before, 2) + mine.shape[2:], part.dtype)
        both = lax.dynamic_update_slice(both, mine, (0, links.own(bit), 0, 0))
        both = lax.dynamic_update_slice(
            both, came.reshape(mine.shape), (0, 1 - links.own(bit), 0, 0)
        )
        self.parts[i] = both.reshape(-1, columns)
        self.known[i] = known + [bit]

    def inside(self, step):
        self.widen(0, self.links.inner[step])

    def cross(self, step):
        links = self.links
        if len(self.parts) == 1:
            half = self.parts[0].shape[1] // 2
            self.parts = [self.parts[0][:, :half], self.parts[0][:, half:]]
            self.known = [self.known[0], self.known[0]]
        orders = ([links.last] + links.upper, links.upper + [links.last])
        for i in range(2):
            self.widen(i, orders[i][step])

    def core(self):
        self.parts += [self.links.swap(part, self.links.core) for part in self.parts]

    def finish(self):
        links = self.links
        before, half = 1 << len(links.upper), self.parts[0].shape[1]
        four = [part.reshape(before, -1, self.rows, half) for part in self.parts]
        wholes, row = [], 0
        for height in self.heights:
            piece = [part[:, :, row : row + height] for part in four]
            own = links.own(links.core)
            whole = jnp.zeros((before, 2) + piece[0].shape[1:3] + (2 * half,), piece[0].dtype)
            for i in range(4):
                place = own if i < 2 else 1 - own
                whole = lax.dynamic_update_slice(
                    whole, piece[i][:, None], (0, place, 0, 0, (i % 2) * half)
                )
            wholes.append(whole.reshape(-1, 2 * half))
            row += height
        return wholes

    def sources(self):
        columns = 2 * self.parts[0].shape[1]
        befores = 1 << len(self.links.upper)
        if len(self.heights) == 1:
            arrays = [part.reshape(befores, -1, part.shape[1]) for part in self.parts]
            return [Source(arrays, 0, arrays[0].shape[1], columns)]
        arrays = [part.reshape(-1, self.rows, part.shape[1]) for part in self.parts]
        sources, row = [], 0
        for height in self.heights:
            sources.append(Source(arrays, row, height, columns))
            row += height
        return sources


class Reduction:
    def __init__(self, links, wide):
        self.links, self.wide = links, wide
        self.terms, self.came = [], []

    def sides(self, left_side, which):
        blocks = 2 << len(self.links.upper)
        wide = left_side.shape[1] // blocks
        chosen = []
        for block in range(0, blocks, 2):
            first = left_side[:, block * wide : (block + 1) * wide]
            second = left_side[:, (block + 1) * wide : (block + 2) * wide]
            chosen.append(jnp.where(which == 0, first, second))
        return jnp.concatenate(chosen, axis=1)

    def send(self, left_side, right_side):
        links = self.links
        away = across(self.sides(left_side, 1 - links.own(links.core)), right_side)
        kept = self.sides(left_side, links.own(links.core))
        self.terms.append(lambda: across(kept, right_side))
        self.came.append(links.swap(away.astype(BF16), links.core))

    def send_rows(self, values):
        links = self.links
        halves = values.reshape(1 << len(links.upper), 2, -1, values.shape[1])
        own = links.own(links.core)
        away = lax.dynamic_index_in_dim(halves, 1 - own, 1, False).reshape(-1, values.shape[1])
        kept = lax.dynamic_index_in_dim(halves, own, 1, False).reshape(-1, values.shape[1])
        self.terms.append(lambda: kept)
        self.came.append(links.swap(away.astype(BF16), links.core))

    def add(self):
        links = self.links
        owners = links.count // 2
        total = []
        for term, came in zip(self.terms, self.came):
            item = (term() + came.astype(F32)).astype(BF16)
            item = item.reshape(owners, -1, item.shape[1])
            for start in range(0, item.shape[2], self.wide):
                total.append(item[:, :, start : start + self.wide])
        total = total[0] if len(total) == 1 else jnp.concatenate(total, axis=1)
        total = total.reshape(-1, total.shape[2])
        half = total.shape[1] // 2
        self.parts = [total[:, :half], total[:, half:]]
        left = [bit for bit in range(links.bits) if bit != links.core]
        self.left = [list(left), list(left)]

    def halve(self, i, bit, out_type=BF16):
        links, part = self.links, self.parts[i]
        columns = part.shape[1]
        before = 1 << sum(1 for other in self.left[i] if other < bit)
        both = part.reshape(before, 2, -1, columns)
        own = links.own(bit)
        away = lax.dynamic_index_in_dim(both, 1 - own, 1, False)
        kept = lax.dynamic_index_in_dim(both, own, 1, False)
        came = links.swap(away.reshape(-1, columns), bit)
        kept = kept.reshape(-1, columns).astype(F32) + came.astype(F32)
        self.parts[i] = kept.astype(out_type)
        self.left[i].remove(bit)

    def cross(self, step):
        links = self.links
        orders = (links.upper + [links.last], [links.last] + links.upper)
        for i in range(2):
            self.halve(i, orders[i][step])

    def join(self, other):
        owners = 1 << len(self.left[0])
        for i in range(2):
            both = [part.reshape(owners, -1, part.shape[1]) for part in (self.parts[i], other.parts[i])]
            self.parts[i] = jnp.concatenate(both, axis=1).reshape(-1, both[0].shape[2])

    def inside(self, step):
        if len(self.parts) == 2:
            self.parts = [jnp.concatenate(self.parts, axis=1)]
        final = step == len(self.links.inner) - 1
        self.halve(0, self.links.inner[-1 - step], F32 if final else BF16)


class Source:
    def __init__(self, arrays, start, height, columns):
        self.arrays, self.start, self.height, self.columns = arrays, start, height, columns


def shampoo(links, matrices, roots):
    side = roots.shape[0]
    big = [roots]
    for source, *_ in matrices:
        for array in source.arrays:
            if not any(array is other for other in big):
                big.append(array)
    place = {id(array): i for i, array in enumerate(big)}
    small, out_shape, scratch, copies = [], [], [], 0
    for source, shard, left_stat, right_stat, root, weight, which in matrices:
        rows, columns = left_stat.shape[1], right_stat.shape[1]
        small += [shard, left_stat, right_stat, root] + ([] if weight is None else [weight])
        out_shape += [
            jax.ShapeDtypeStruct(left_stat.shape, F32),
            jax.ShapeDtypeStruct(right_stat.shape, F32),
            jax.ShapeDtypeStruct(
                (right_stat.shape[0], rows) if weight is None else weight.shape,
                BF16 if weight is None else F32,
            ),
        ]
        if len(source.arrays) == 1:
            scratch.append(pltpu.VMEM((1, rows, columns), BF16))
            copies += 1
        else:
            blocks = 2 * source.arrays[0].shape[0]
            scratch.append(pltpu.VMEM((blocks, rows // blocks, columns), BF16))
            copies += 4 << len(links.upper)
        scratch.append(pltpu.VMEM((side, side), BF16))
        copies += 1
    bits = jnp.stack([links.index, links.own(links.core)]).astype(jnp.int32)

    def kernel(*refs):
        place_ref, refs = refs[0], list(refs[1:])
        bigs, refs = refs[: len(big)], refs[len(big) :]
        smalls, refs = refs[: len(small)], refs[len(small) :]
        outs, refs = refs[: len(out_shape)], refs[len(out_shape) :]
        scratches, done = refs[: len(scratch)], refs[-1]
        index, own = place_ref[0], place_ref[1]
        started, used = [], 0
        for i, (source, *_, which) in enumerate(matrices):
            whole, root = scratches[2 * i], scratches[2 * i + 1]
            mine = []
            if len(source.arrays) == 1:
                ref = bigs[place[id(source.arrays[0])]]
                mine.append((ref.at[:, pl.ds(source.start, source.columns)], whole.at[0]))
            else:
                befores = 1 << len(links.upper)
                deep = source.arrays[0].shape[0] // befores
                half = source.arrays[0].shape[2]
                for part in range(4):
                    ref = bigs[place[id(source.arrays[part])]]
                    core = own if part < 2 else 1 - own
                    for before in range(befores):
                        mine.append(
                            (
                                ref.at[
                                    pl.ds(before * deep, deep), pl.ds(source.start, source.height)
                                ],
                                whole.at[
                                    pl.ds((2 * before + core) * deep, deep),
                                    :,
                                    pl.ds((part % 2) * half, half),
                                ],
                            )
                        )
            mine.append((bigs[0].at[:, pl.ds(which * side, side)], root))
            group = []
            for from_ref, to_ref in mine:
                copy = pltpu.make_async_copy(from_ref, to_ref, done.at[used])
                copy.start()
                group.append(copy)
                used += 1
            started.append(group)
        for i, (source, shard, left_stat, right_stat, root, weight, which) in enumerate(matrices):
            for copy in started[i]:
                copy.wait()
            rows, columns = left_stat.shape[1], right_stat.shape[1]
            high, wide = left_stat.shape[0], right_stat.shape[0]
            whole = scratches[2 * i][...].reshape(rows, columns)
            shard_ref, left_ref, right_ref, root_ref = smalls[:4]
            lane = lax.broadcasted_iota(jnp.int32, (wide, columns), 1)
            row = lax.broadcasted_iota(jnp.int32, (wide, columns), 0)
            pick = (lane == row + index * wide).astype(F32)
            stacked = [shard_ref[...], pick] + ([root_ref[...]] if weight is None else [])
            first = against(jnp.concatenate(stacked, axis=0).astype(BF16), whole)
            outs[3 * i][...] = 0.5 * left_ref[...] + (0.5 / columns) * first[:high]
            picked = first[high : high + wide]
            other = scratches[2 * i + 1][...]
            if weight is None:
                second = product(picked.astype(BF16), whole)
                outs[3 * i + 1][...] = 0.5 * right_ref[...] + (0.5 / rows) * second
                turned = first[high + wide :].astype(BF16)
                outs[3 * i + 2][...] = product(turned, other).astype(BF16)
                smalls = smalls[4:]
            else:
                second = product(
                    jnp.concatenate([root_ref[...], picked], axis=0).astype(BF16), whole
                )
                outs[3 * i + 1][...] = 0.5 * right_ref[...] + (0.5 / rows) * second[high:]
                step = product(second[:high].astype(BF16), other)
                outs[3 * i + 2][...] = smalls[4][...] - step * (1.0 / math.sqrt(rows))
                smalls = smalls[5:]

    vmem = pl.BlockSpec(memory_space=pltpu.VMEM)
    results = pl.pallas_call(
        kernel,
        out_shape=out_shape,
        in_specs=[pl.BlockSpec(memory_space=pltpu.SMEM)]
        + [pl.BlockSpec(memory_space=pl.ANY)] * len(big)
        + [vmem] * len(small),
        out_specs=[vmem] * len(out_shape),
        scratch_shapes=scratch + [pltpu.SemaphoreType.DMA((copies,))],
        compiler_params=pltpu.CompilerParams(vmem_limit_bytes=56 << 20),
    )(bits, *big, *small)
    return [results[3 * i : 3 * i + 3] for i in range(len(matrices))]


def body(
    embedding,
    latent,
    segment_ids,
    cotangent,
    weight_adapt,
    weight_attn,
    weight_gateup,
    weight_down,
    norm_gains,
    left_adapt,
    right_adapt,
    left_attn,
    right_attn,
    left_gateup,
    right_gateup,
    left_down,
    right_down,
    left_root_adapt,
    right_root_adapt,
    left_root_attn,
    right_root_attn,
    left_root_gateup,
    right_root_gateup,
    left_root_down,
    right_root_down,
    gain_moment,
):
    n_dp, n_seq = lax.axis_size("dp"), lax.axis_size("seq")
    links = Links(n_dp, n_seq)
    seq_count, group_len, width = embedding.shape
    tokens = seq_count * group_len
    length = group_len * n_seq
    hidden_width = weight_gateup.shape[2]
    by_heads = HEADS % n_seq == 0

    gateup_rows = weight_gateup.astype(BF16)
    down_rows = weight_down.astype(BF16).reshape(-1, hidden_width)
    feed_full = lax.all_gather(
        jnp.concatenate([gateup_rows[0], gateup_rows[1], down_rows], axis=1),
        AXES,
        axis=0,
        tiled=True,
    )
    gain_share = norm_gains.shape[1]
    small = jnp.concatenate(
        [norm_gains.astype(BF16).reshape(-1), segment_ids.astype(BF16).reshape(-1)]
    )
    small = jnp.pad(small[None], ((0, 7), (0, width - small.shape[0])))
    attn_rows = weight_attn.astype(BF16)
    first = Gathering(links, [weight_adapt.astype(BF16), small])
    second = Gathering(links, [attn_rows[i] for i in range(4)])
    inner_steps, cross_steps = range(len(links.inner)), range(links.steps)
    for step in inner_steps:
        first.inside(step)
    tick([first, second])
    for step in inner_steps:
        second.inside(step)
    for step in cross_steps:
        first.cross(step)
    tick([first, second])
    first.core()
    adapt_full, small = first.finish()
    for step in cross_steps:
        second.cross(step)
    second.core()
    query_full, key_full, value_full, out_full = second.finish()

    small = small.reshape(links.count, 8, width)[:, 0]
    gain_values = small[:, : 4 * gain_share].reshape(links.count, 4, gain_share)
    gain_values = gain_values.transpose(1, 0, 2).reshape(4, width).astype(F32)
    ids = small[:, 4 * gain_share : 4 * gain_share + tokens].reshape(n_dp, n_seq, seq_count, -1)
    ids = lax.dynamic_index_in_dim(ids, lax.axis_index("dp"), 0, False)
    segment_whole = ids.transpose(1, 0, 2).reshape(seq_count, length).astype(jnp.int32)

    all_places = jnp.arange(length, dtype=jnp.int32)
    doc_starts = jnp.sum(
        (segment_whole[:, None, :] < segment_whole[:, :, None]).astype(jnp.int32), axis=2
    )
    places = all_places[None, :] - doc_starts
    half_dim = HEAD_DIM // 2
    frequency = THETA ** (-jnp.arange(half_dim, dtype=F32) / half_dim)
    angles = places.astype(F32)[..., None] * frequency
    cosine_all, sine_all = jnp.cos(angles), jnp.sin(angles)
    own_start = links.seq_index * group_len
    cosine = lax.dynamic_slice_in_dim(cosine_all, own_start, group_len, 1)
    sine_table = lax.dynamic_slice_in_dim(sine_all, own_start, group_len, 1)
    if by_heads:
        query_places, segment_query = all_places, segment_whole
        cosine_back, sine_back = cosine_all[:, None], sine_all[:, None]
    else:
        query_places, segment_query = own_start + jnp.arange(group_len), segment_ids
        cosine_back, sine_back = cosine[:, None], sine_table[:, None]
    allowed = (all_places[None, None, :] <= query_places[None, :, None]) & (
        segment_whole[:, None, :] == segment_query[:, :, None]
    )

    def to_heads(values):
        parts = values.shape[2]
        values = values.transpose(3, 2, 0, 1, 4)
        came = lax.all_to_all(values, "seq", 0, 0, tiled=True)
        came = came.reshape(n_seq, HEADS // n_seq, parts, seq_count, group_len, HEAD_DIM)
        came = came.transpose(2, 3, 1, 0, 4, 5)
        return came.reshape(parts, seq_count, HEADS // n_seq, length, HEAD_DIM)

    def to_tokens(values):
        parts = values.shape[0]
        own = HEADS // n_seq
        values = values.reshape(parts, seq_count, own, n_seq, group_len, HEAD_DIM)
        values = values.transpose(3, 2, 0, 1, 4, 5)
        came = lax.all_to_all(values, "seq", 0, 0, tiled=True)
        came = came.reshape(HEADS, parts, seq_count, group_len, HEAD_DIM)
        return came.transpose(1, 2, 3, 0, 4)

    scaling = 1.0 / math.sqrt(HEAD_DIM)

    def attention(queries, keys, values, with_feed):
        if by_heads:
            queries, keys, values = to_heads(jnp.stack([queries, keys, values], axis=2))
        else:
            queries = queries.transpose(0, 2, 1, 3)
            keys, values = (
                lax.all_gather(item, "seq", axis=1, tiled=True).transpose(0, 2, 1, 3)
                for item in (keys, values)
            )
        if with_feed:
            queries, feed[0], feed[1] = tie(queries, feed[0], feed[1])
        scores = jnp.einsum("shqd,shkd->shqk", queries, keys, preferred_element_type=F32)
        scores = jnp.where(allowed[:, None], scores * scaling, -1e30)
        exponent = jnp.exp(scores - jnp.max(scores, axis=-1, keepdims=True))
        soft_full = exponent / jnp.sum(exponent, axis=-1, keepdims=True)
        mixed = jnp.einsum(
            "shqk,shkd->shqd", soft_full.astype(BF16), values, preferred_element_type=F32
        ).astype(BF16)
        if by_heads:
            mixed = to_tokens(mixed[None])[0]
        else:
            mixed = mixed.transpose(0, 2, 1, 3)
        return mixed.reshape(tokens, width), (queries, keys, values, soft_full)

    def attention_back(mixed_grad, saved):
        queries, keys, values, soft_full = saved
        soft_grad = jnp.einsum("shqd,shkd->shqk", mixed_grad, values, preferred_element_type=F32)
        inner_sum = jnp.sum(soft_full * soft_grad, axis=-1, keepdims=True)
        score_grad = (soft_full * (soft_grad - inner_sum)).astype(BF16)
        query_grad = (
            jnp.einsum("shqk,shkd->shqd", score_grad, keys, preferred_element_type=F32) * scaling
        )
        key_grad = (
            jnp.einsum("shqk,shqd->shkd", score_grad, queries, preferred_element_type=F32)
            * scaling
        )
        value_grad = jnp.einsum(
            "shqk,shqd->shkd", soft_full.astype(BF16), mixed_grad, preferred_element_type=F32
        )
        if by_heads:
            query_grad = rotate(query_grad, cosine_back, -sine_back).astype(BF16)
            key_grad = rotate(key_grad, cosine_back, -sine_back).astype(BF16)
            value_grad = value_grad.astype(BF16)
            return jnp.stack([query_grad, key_grad, value_grad])
        key_grad, value_grad = (
            lax.psum_scatter(item.astype(BF16), "seq", scatter_dimension=2, tiled=True).astype(F32)
            for item in (key_grad, value_grad)
        )
        query_grad = rotate(query_grad, cosine_back, -sine_back).astype(BF16)
        key_grad = rotate(key_grad, cosine_back, -sine_back).astype(BF16)
        grads = jnp.stack([query_grad, key_grad, value_grad.astype(BF16)])
        return grads.transpose(0, 1, 3, 2, 4)

    embed_flat = embedding.reshape(tokens, width)
    embed_part = product(embed_flat, adapt_full[width:])
    embed_part, feed_full = tie(embed_part, feed_full)
    feed = [
        feed_full[:, : 2 * hidden_width],
        feed_full[:, 2 * hidden_width :].reshape(hidden_width, width),
    ]

    roots = []

    def forward(latent_low, with_roots=False):
        start_sum = product(latent_low, adapt_full[:width]) + embed_part
        scale_one = norm_scale(start_sum)
        normed_one = (start_sum * scale_one * gain_values[0]).astype(BF16)
        head_shape = (seq_count, group_len, HEADS, HEAD_DIM)
        turn_cos, turn_sin = cosine[:, :, None, :], sine_table[:, :, None, :]
        queries = product(normed_one, query_full).reshape(head_shape)
        queries = rotate(queries, turn_cos, turn_sin).astype(BF16)
        keys = product(normed_one, key_full).reshape(head_shape)
        keys = rotate(keys, turn_cos, turn_sin).astype(BF16)
        values = product(normed_one, value_full).astype(BF16).reshape(head_shape)
        mixed_heads, attended = attention(queries, keys, values, with_roots)
        if with_roots:
            root_stack = jnp.concatenate(
                [
                    right_root_adapt.astype(BF16)[:, None],
                    right_root_attn.astype(BF16).transpose(1, 0, 2),
                    right_root_down.astype(BF16)[:, None],
                    left_root_gateup.astype(BF16).transpose(1, 0, 2),
                ],
                axis=1,
            )
            share = root_stack.shape[0]
            root_stack, mixed_heads = tie(root_stack.reshape(share, 8 * width), mixed_heads)
            roots.append(lax.all_gather(root_stack, AXES, axis=0, tiled=True))
        branch = product(mixed_heads, out_full)
        scale_two = norm_scale(branch)
        middle = start_sum + branch * scale_two * gain_values[1]
        scale_three = norm_scale(middle)
        normed_three = (middle * scale_three * gain_values[2]).astype(BF16)
        gateup_full, down_full = feed
        both = product(normed_three, gateup_full)
        gate_value, upward = both[:, :hidden_width], both[:, hidden_width:]
        hidden = (jax.nn.silu(gate_value) * upward).astype(BF16)
        feed_out = product(hidden, down_full)
        scale_four = norm_scale(feed_out)
        result = middle + feed_out * scale_four * gain_values[3]
        saved_values = (
            start_sum,
            scale_one,
            normed_one,
            attended,
            mixed_heads,
            branch,
            scale_two,
            middle,
            scale_three,
            normed_three,
            gate_value,
            upward,
            hidden,
            feed_out,
            scale_four,
        )
        return (result, saved_values)

    latent_low = latent.reshape(tokens, width)
    latent_state, unused_saved = forward(latent_low, True)
    latent_low = latent_state.astype(BF16)
    final_state, saved_values = forward(latent_low)
    (
        start_sum,
        scale_one,
        normed_one,
        attended,
        mixed_heads,
        branch,
        scale_two,
        middle,
        scale_three,
        normed_three,
        gate_value,
        upward,
        hidden,
        feed_out,
        scale_four,
    ) = saved_values
    factor = 1.0 / math.sqrt(seq_count * n_dp * length)
    incoming = cotangent.astype(F32).reshape(tokens, width)
    feed_grad, gain_four = norm_back(feed_out, scale_four, gain_values[3], incoming)
    feed_grad = feed_grad.astype(BF16)
    down_sum = Reduction(links, width)
    down_sum.send(hidden, feed_grad)
    gateup_full, down_full = feed
    hidden_grad = against(feed_grad, down_full)
    gate_grad = (hidden_grad * upward * silu_grad(gate_value)).astype(BF16)
    up_grad = (hidden_grad * jax.nn.silu(gate_value)).astype(BF16)
    gateup_sum = Reduction(links, hidden_width)
    gateup_sum.send(normed_three, gate_grad)
    gateup_sum.send(normed_three, up_grad)
    both_grad = jnp.concatenate([gate_grad, up_grad], axis=1)
    normed_three_grad = against(both_grad, gateup_full)
    middle_grad, gain_three = norm_back(middle, scale_three, gain_values[2], normed_three_grad)
    middle_grad = middle_grad + incoming
    branch_grad, gain_two = norm_back(branch, scale_two, gain_values[1], middle_grad)
    branch_grad = branch_grad.astype(BF16)
    mixed_grad = against(branch_grad, out_full).astype(BF16)
    rest_sum = Reduction(links, width)
    rest_sum.send(mixed_heads, branch_grad)
    down_sum.add()
    (mixed_grad,) = tick([down_sum], mixed_grad)
    mixed_grad = mixed_grad.reshape(seq_count, group_len, HEADS, HEAD_DIM)
    if by_heads:
        mixed_grad = to_heads(mixed_grad[:, :, None])[0]
    else:
        mixed_grad = mixed_grad.transpose(0, 2, 1, 3)
    down_sum.cross(0)
    gateup_sum.add()
    (mixed_grad,) = tick([down_sum, gateup_sum], mixed_grad)
    grads = attention_back(mixed_grad, attended)
    for step in cross_steps[1:]:
        down_sum.cross(step)
    gateup_sum.cross(0)
    if by_heads:
        grads = to_tokens(grads)
    query_pre, key_pre, value_pre = grads.reshape(3, tokens, width)
    query_pre, key_pre, value_pre = tick([down_sum, gateup_sum], query_pre, key_pre, value_pre)
    for step in cross_steps[1:]:
        gateup_sum.cross(step)
    rest_sum.send(normed_one, jnp.concatenate([query_pre, key_pre, value_pre], axis=1))
    normed_one_grad = (
        against(query_pre, query_full) + against(key_pre, key_full) + against(value_pre, value_full)
    )
    start_grad, gain_one = norm_back(start_sum, scale_one, gain_values[0], normed_one_grad)
    start_grad = (start_grad + middle_grad).astype(BF16)
    joined = jnp.concatenate([latent_low, embed_flat], axis=1)
    rest_sum.send(joined, start_grad)
    gain_sums = jnp.stack([gain_one, gain_two, gain_three, gain_four])
    gain_sums = gain_sums.reshape(4, links.count, gain_share).transpose(1, 0, 2)
    gain_sums = gain_sums.reshape(links.count, 1, 4 * gain_share)
    gain_sums = jnp.pad(gain_sums, ((0, 0), (0, 7), (0, width - 4 * gain_share)))
    rest_sum.send_rows(gain_sums.reshape(-1, width))
    rest_sum.add()
    start_grad, root_rows = tick([gateup_sum, down_sum, rest_sum], start_grad, roots[0])
    rest_sum.cross(0)
    for step in inner_steps:
        down_sum.inside(step)
    for step in inner_steps:
        gateup_sum.inside(step)
    tick([rest_sum, gateup_sum, down_sum])
    reduced_down = down_sum.parts[0] * factor
    first = Gathering(links, [reduced_down.astype(BF16)])
    left_root_adapt, left_root_attn, left_root_down, right_root_gateup, reduced_down = tie(
        left_root_adapt, left_root_attn, left_root_down, right_root_gateup, reduced_down
    )
    for step in cross_steps[1:]:
        rest_sum.cross(step)
    gate_shards = (gateup_sum.parts[0] * factor).reshape(2, -1, hidden_width)
    full_both = lax.all_gather(
        jnp.concatenate([gate_shards[0], gate_shards[1]], axis=1).astype(BF16),
        AXES,
        axis=0,
        tiled=True,
    )
    first.inside(0)
    tick([rest_sum, first])
    rest_sum.inside(0)
    for step in inner_steps[1:]:
        first.inside(step)
    tick([rest_sum, first])
    for step in inner_steps[1:]:
        rest_sum.inside(step)
    first.cross(0)
    tick([rest_sum, first])
    reduced_rest = rest_sum.parts[0] * factor
    row_share = width // links.count
    attn_shards = reduced_rest[: 4 * row_share].reshape(4, row_share, width)
    attn_shards = jnp.concatenate([attn_shards[1:], attn_shards[:1]], axis=0)
    reduced_adapt = reduced_rest[4 * row_share : 6 * row_share]
    reduced_gains = reduced_rest[6 * row_share, : 4 * gain_share].reshape(4, gain_share)
    third = Gathering(
        links, [attn_shards[i].astype(BF16) for i in range(4)] + [reduced_adapt.astype(BF16)]
    )
    third.inside(0)
    for step in cross_steps[1:]:
        first.cross(step)
    tick([third, first])
    for step in inner_steps[1:]:
        third.inside(step)
    first.core()
    tick([third, first])
    third.cross(0)
    tick([third])
    for step in cross_steps[1:]:
        third.cross(step)
    tick([third])
    third.core()
    tick([third])
    grad_embedding = against(start_grad, adapt_full[width:]).reshape(
        seq_count, group_len, width
    )
    def statistics(shard, whole, left_stat, right_stat, left_root):
        rows, columns = whole.shape
        new_left = 0.5 * left_stat + (0.5 / columns) * against(shard.astype(BF16), whole)
        count = right_stat.shape[0]
        own = lax.dynamic_slice_in_dim(whole, links.index * count, count, 1).T
        if left_root is None:
            return (new_left, 0.5 * right_stat + (0.5 / rows) * product(own, whole), None)
        own_count = left_root.shape[0]
        both = product(jnp.concatenate([left_root.astype(BF16), own], axis=0), whole)
        return (new_left, 0.5 * right_stat + (0.5 / rows) * both[own_count:], both[:own_count])

    def step(part, which, rows):
        root = root_rows[:, which * width : (which + 1) * width]
        return product(part.astype(BF16), root) * (1.0 / math.sqrt(rows))

    fits = row_share % 16 == 0
    if fits:
        gateup_parts = shampoo(
            links,
            [
                (
                    Source([full_both], i * hidden_width, width, hidden_width),
                    gate_shards[i],
                    left_gateup[i],
                    right_gateup[i],
                    right_root_gateup[i],
                    None,
                    6 + i,
                )
                for i in range(2)
            ],
            root_rows,
        )
        step_columns = jnp.stack([member[2].T for member in gateup_parts])
    else:
        whole_gates = [full_both[:, :hidden_width], full_both[:, hidden_width:]]
        gateup_parts = [
            statistics(gate_shards[i], whole_gates[i], left_gateup[i], right_gateup[i], None)
            for i in range(2)
        ]
        step_columns = []
        for i in range(2):
            turned = against(whole_gates[i], right_root_gateup[i].astype(BF16)).astype(BF16)
            root = root_rows[:, (6 + i) * width : (7 + i) * width]
            step_columns.append(product(root, turned).astype(BF16))
        step_columns = jnp.stack(step_columns)
    ff_share = step_columns.shape[2]
    step_columns = step_columns.reshape(2, links.count, row_share, ff_share).transpose(1, 0, 2, 3)
    step_rows = lax.all_to_all(step_columns, AXES, 0, 0, tiled=True)
    step_gateup = step_rows.transpose(1, 2, 0, 3).reshape(2, row_share, hidden_width)
    new_gateup = weight_gateup - step_gateup.astype(F32) * (1.0 / math.sqrt(width))

    if fits:
        ((new_left_down, new_right_down, new_down),) = shampoo(
            links,
            [
                (
                    first.sources()[0],
                    reduced_down,
                    left_down,
                    right_down,
                    left_root_down,
                    weight_down,
                    5,
                )
            ],
            root_rows,
        )
        sources = third.sources()
        attn_parts = [
            (
                sources[i],
                attn_shards[i],
                left_attn[i],
                right_attn[i],
                left_root_attn[i],
                weight_attn[i],
                1 + i,
            )
            for i in range(4)
        ]
        adapt_part = (
            sources[4],
            reduced_adapt,
            left_adapt,
            right_adapt,
            left_root_adapt,
            weight_adapt,
            0,
        )
        *attn_parts, (new_left_adapt, new_right_adapt, new_adapt) = shampoo(
            links, attn_parts + [adapt_part], root_rows
        )
        new_attn = jnp.stack([member[2] for member in attn_parts])
    else:
        (full_down,) = first.finish()
        *attn_wholes, full_adapt = third.finish()
        new_left_down, new_right_down, down_part = statistics(
            reduced_down, full_down, left_down, right_down, left_root_down
        )
        new_down = weight_down - step(down_part, 5, hidden_width)
        attn_parts = [
            statistics(
                attn_shards[i], attn_wholes[i], left_attn[i], right_attn[i], left_root_attn[i]
            )
            for i in range(4)
        ]
        new_attn = weight_attn - jnp.stack(
            [step(attn_parts[i][2], 1 + i, width) for i in range(4)]
        )
        new_left_adapt, new_right_adapt, adapt_part = statistics(
            reduced_adapt, full_adapt, left_adapt, right_adapt, left_root_adapt
        )
        new_adapt = weight_adapt - step(adapt_part, 0, 2 * width)
    new_gain_moment = 0.5 * gain_moment + 0.5 * reduced_gains * reduced_gains
    new_norm_gains = norm_gains - 0.5 * reduced_gains / (jnp.sqrt(new_gain_moment) + 1e-08)
    latent_out = final_state.reshape(seq_count, group_len, width).astype(BF16)
    return (
        latent_out,
        grad_embedding,
        reduced_adapt,
        attn_shards,
        gate_shards,
        reduced_down,
        reduced_gains,
        new_left_adapt,
        new_right_adapt,
        jnp.stack([member[0] for member in attn_parts]),
        jnp.stack([member[1] for member in attn_parts]),
        jnp.stack([member[0] for member in gateup_parts]),
        jnp.stack([member[1] for member in gateup_parts]),
        new_left_down,
        new_right_down,
        new_adapt,
        new_attn,
        new_gateup,
        new_down,
        new_gain_moment,
        new_norm_gains,
    )

def solution(mesh):
    return jax.shard_map(
        body,
        mesh=mesh,
        in_specs=(
            P("dp", "seq", None),
            P("dp", "seq", None),
            P("dp", "seq"),
            P("dp", "seq", None),
            P(("dp", "seq"), None),
            P(None, ("dp", "seq"), None),
            P(None, ("dp", "seq"), None),
            P(("dp", "seq"), None),
            P(None, ("dp", "seq")),
            P(("dp", "seq"), None),
            P(("dp", "seq"), None),
            P(None, ("dp", "seq"), None),
            P(None, ("dp", "seq"), None),
            P(None, ("dp", "seq"), None),
            P(None, ("dp", "seq"), None),
            P(("dp", "seq"), None),
            P(("dp", "seq"), None),
            P(("dp", "seq"), None),
            P(("dp", "seq"), None),
            P(None, ("dp", "seq"), None),
            P(None, ("dp", "seq"), None),
            P(None, ("dp", "seq"), None),
            P(None, ("dp", "seq"), None),
            P(("dp", "seq"), None),
            P(("dp", "seq"), None),
            P(None, ("dp", "seq")),
        ),
        out_specs=(
            P("dp", "seq", None),
            P("dp", "seq", None),
            P(("dp", "seq"), None),
            P(None, ("dp", "seq"), None),
            P(None, ("dp", "seq"), None),
            P(("dp", "seq"), None),
            P(None, ("dp", "seq")),
            P(("dp", "seq"), None),
            P(("dp", "seq"), None),
            P(None, ("dp", "seq"), None),
            P(None, ("dp", "seq"), None),
            P(None, ("dp", "seq"), None),
            P(None, ("dp", "seq"), None),
            P(("dp", "seq"), None),
            P(("dp", "seq"), None),
            P(("dp", "seq"), None),
            P(None, ("dp", "seq"), None),
            P(None, ("dp", "seq"), None),
            P(("dp", "seq"), None),
            P(None, ("dp", "seq")),
            P(None, ("dp", "seq")),
        ),
        check_vma=False,
    )
```

```python
import math

import jax
import jax.numpy as jnp
from jax import lax
from jax.experimental import pallas as pl
from jax.experimental.pallas import tpu as pltpu
from jax.sharding import PartitionSpec as P

HEADS = 8
HEAD_DIM = 128
EPSILON = 1e-06
THETA = 50000.0
AXES = ("dp", "seq")
BF16 = jnp.bfloat16
F32 = jnp.float32


def product(left_side, right_side):
    return jnp.dot(left_side, right_side, preferred_element_type=F32)


def across(left_side, right_side):
    return lax.dot_general(
        left_side, right_side, (((0,), (0,)), ((), ())), preferred_element_type=F32
    )


def against(left_side, right_side):
    return lax.dot_general(
        left_side, right_side, (((1,), (1,)), ((), ())), preferred_element_type=F32
    )


def norm_scale(values):
    return lax.rsqrt(jnp.mean(values * values, axis=-1, keepdims=True) + EPSILON)


def norm_back(values, scaling, gain_row, gradient):
    unit_rows = values * scaling
    weighted = gradient * gain_row
    moved = scaling * (
        weighted - unit_rows * jnp.mean(unit_rows * weighted, axis=-1, keepdims=True)
    )
    return (moved, jnp.sum(gradient * unit_rows, axis=0))


def rotate(values, cosine, sine_table):
    half_dim = values.shape[-1] // 2
    first_half = values[..., :half_dim]
    second_half = values[..., half_dim:]
    return jnp.concatenate(
        [
            first_half * cosine - second_half * sine_table,
            second_half * cosine + first_half * sine_table,
        ],
        axis=-1,
    )


def silu_grad(values):
    sigmoid_value = jax.nn.sigmoid(values)
    return sigmoid_value * (1.0 + values * (1.0 - sigmoid_value))


def tie(*values):
    return lax.optimization_barrier(values)


def tick(works, *values):
    flat = [part for work in works for part in work.parts]
    tied = list(lax.optimization_barrier(tuple(flat) + values))
    for work in works:
        count = len(work.parts)
        work.parts, tied = tied[:count], tied[count:]
    return tied


class Links:
    def __init__(self, n_dp, n_seq):
        self.count = n_dp * n_seq
        self.bits = (self.count - 1).bit_length()
        self.core = (n_dp - 1).bit_length() - 1
        self.last = self.bits - 1
        self.upper = list(range(self.core))
        self.inner = list(range(self.core + 1, self.last))
        self.index = lax.axis_index("dp") * n_seq + lax.axis_index("seq")
        self.seq_index = lax.axis_index("seq")
        self.pairs = [
            [(i, i ^ (1 << (self.bits - 1 - bit))) for i in range(self.count)]
            for bit in range(self.bits)
        ]
        self.steps = len(self.upper) + 1

    def own(self, bit):
        return (self.index >> (self.bits - 1 - bit)) & 1

    def swap(self, values, bit):
        return lax.ppermute(values, AXES, self.pairs[bit])


class Gathering:
    def __init__(self, links, shards):
        self.links = links
        self.heights = [shard.shape[0] for shard in shards]
        self.rows = sum(self.heights)
        shard = shards[0] if len(shards) == 1 else jnp.concatenate(shards, axis=0)
        self.parts = [shard]
        self.known = [[]]

    def widen(self, i, bit):
        links, part, known = self.links, self.parts[i], self.known[i]
        came = links.swap(part, bit)
        columns = part.shape[1]
        before = 1 << sum(1 for other in known if other < bit)
        mine = part.reshape(before, 1, -1, columns)
        both = jnp.zeros((before, 2) + mine.shape[2:], part.dtype)
        both = lax.dynamic_update_slice(both, mine, (0, links.own(bit), 0, 0))
        both = lax.dynamic_update_slice(
            both, came.reshape(mine.shape), (0, 1 - links.own(bit), 0, 0)
        )
        self.parts[i] = both.reshape(-1, columns)
        self.known[i] = known + [bit]

    def inside(self, step):
        self.widen(0, self.links.inner[step])

    def cross(self, step):
        links = self.links
        if len(self.parts) == 1:
            half = self.parts[0].shape[1] // 2
            self.parts = [self.parts[0][:, :half], self.parts[0][:, half:]]
            self.known = [self.known[0], self.known[0]]
        orders = ([links.last] + links.upper, links.upper + [links.last])
        for i in range(2):
            self.widen(i, orders[i][step])

    def core(self):
        self.parts += [self.links.swap(part, self.links.core) for part in self.parts]

    def finish(self):
        links = self.links
        before, half = 1 << len(links.upper), self.parts[0].shape[1]
        four = [part.reshape(before, -1, self.rows, half) for part in self.parts]
        wholes, row = [], 0
        for height in self.heights:
            piece = [part[:, :, row : row + height] for part in four]
            own = links.own(links.core)
            whole = jnp.zeros((before, 2) + piece[0].shape[1:3] + (2 * half,), piece[0].dtype)
            for i in range(4):
                place = own if i < 2 else 1 - own
                whole = lax.dynamic_update_slice(
                    whole, piece[i][:, None], (0, place, 0, 0, (i % 2) * half)
                )
            wholes.append(whole.reshape(-1, 2 * half))
            row += height
        return wholes

    def sources(self):
        columns = 2 * self.parts[0].shape[1]
        befores = 1 << len(self.links.upper)
        if len(self.heights) == 1:
            arrays = [part.reshape(befores, -1, part.shape[1]) for part in self.parts]
            return [Source(arrays, 0, arrays[0].shape[1], columns)]
        arrays = [part.reshape(-1, self.rows, part.shape[1]) for part in self.parts]
        sources, row = [], 0
        for height in self.heights:
            sources.append(Source(arrays, row, height, columns))
            row += height
        return sources


class Reduction:
    def __init__(self, links, wide):
        self.links, self.wide = links, wide
        self.terms, self.came = [], []

    def sides(self, left_side, which):
        blocks = 2 << len(self.links.upper)
        wide = left_side.shape[1] // blocks
        chosen = []
        for block in range(0, blocks, 2):
            first = left_side[:, block * wide : (block + 1) * wide]
            second = left_side[:, (block + 1) * wide : (block + 2) * wide]
            chosen.append(jnp.where(which == 0, first, second))
        return jnp.concatenate(chosen, axis=1)

    def send(self, left_side, right_side):
        links = self.links
        away = across(self.sides(left_side, 1 - links.own(links.core)), right_side)
        kept = self.sides(left_side, links.own(links.core))
        self.terms.append(lambda: across(kept, right_side))
        self.came.append(links.swap(away.astype(BF16), links.core))

    def send_rows(self, values):
        links = self.links
        halves = values.reshape(1 << len(links.upper), 2, -1, values.shape[1])
        own = links.own(links.core)
        away = lax.dynamic_index_in_dim(halves, 1 - own, 1, False).reshape(-1, values.shape[1])
        kept = lax.dynamic_index_in_dim(halves, own, 1, False).reshape(-1, values.shape[1])
        self.terms.append(lambda: kept)
        self.came.append(links.swap(away.astype(BF16), links.core))

    def add(self):
        links = self.links
        owners = links.count // 2
        total = []
        for term, came in zip(self.terms, self.came):
            item = (term() + came.astype(F32)).astype(BF16)
            item = item.reshape(owners, -1, item.shape[1])
            for start in range(0, item.shape[2], self.wide):
                total.append(item[:, :, start : start + self.wide])
        total = total[0] if len(total) == 1 else jnp.concatenate(total, axis=1)
        total = total.reshape(-1, total.shape[2])
        half = total.shape[1] // 2
        self.parts = [total[:, :half], total[:, half:]]
        left = [bit for bit in range(links.bits) if bit != links.core]
        self.left = [list(left), list(left)]

    def halve(self, i, bit, out_type=BF16):
        links, part = self.links, self.parts[i]
        columns = part.shape[1]
        before = 1 << sum(1 for other in self.left[i] if other < bit)
        both = part.reshape(before, 2, -1, columns)
        own = links.own(bit)
        away = lax.dynamic_index_in_dim(both, 1 - own, 1, False)
        kept = lax.dynamic_index_in_dim(both, own, 1, False)
        came = links.swap(away.reshape(-1, columns), bit)
        kept = kept.reshape(-1, columns).astype(F32) + came.astype(F32)
        self.parts[i] = kept.astype(out_type)
        self.left[i].remove(bit)

    def cross(self, step):
        links = self.links
        orders = (links.upper + [links.last], [links.last] + links.upper)
        for i in range(2):
            self.halve(i, orders[i][step])

    def join(self, other):
        owners = 1 << len(self.left[0])
        for i in range(2):
            both = [part.reshape(owners, -1, part.shape[1]) for part in (self.parts[i], other.parts[i])]
            self.parts[i] = jnp.concatenate(both, axis=1).reshape(-1, both[0].shape[2])

    def inside(self, step):
        if len(self.parts) == 2:
            self.parts = [jnp.concatenate(self.parts, axis=1)]
        final = step == len(self.links.inner) - 1
        self.halve(0, self.links.inner[-1 - step], F32 if final else BF16)


class Source:
    def __init__(self, arrays, start, height, columns):
        self.arrays, self.start, self.height, self.columns = arrays, start, height, columns


def shampoo(links, groups, roots):
    side = roots.shape[0]
    befores = 1 << len(links.upper)
    big = [roots]
    for sources, *_ in groups:
        for source in sources:
            for array in source.arrays:
                if not any(array is other for other in big):
                    big.append(array)
    place = {id(array): i for i, array in enumerate(big)}
    small, out_shape, scratch, copies = [], [], [], 0
    for sources, shards, left_stats, right_stats, own_roots, weights, which in groups:
        count, _, rows = left_stats.shape
        columns = right_stats.shape[2]
        small += [shards, left_stats, right_stats, own_roots]
        small += [] if weights is None else [weights]
        third = (count, right_stats.shape[1], rows) if weights is None else weights.shape
        out_shape += [
            jax.ShapeDtypeStruct(left_stats.shape, F32),
            jax.ShapeDtypeStruct(right_stats.shape, F32),
            jax.ShapeDtypeStruct(third, BF16 if weights is None else F32),
        ]
        for source in sources:
            if len(source.arrays) == 1:
                scratch.append(pltpu.VMEM((1, rows, columns), BF16))
                copies += 2
            else:
                blocks = 2 * source.arrays[0].shape[0]
                scratch.append(pltpu.VMEM((blocks, rows // blocks, columns), BF16))
                copies += 4 * befores + 1
            scratch.append(pltpu.VMEM((side, side), BF16))
    bits = jnp.stack([links.index, links.own(links.core)]).astype(jnp.int32)

    def kernel(*refs):
        place_ref, refs = refs[0], list(refs[1:])
        bigs, refs = refs[: len(big)], refs[len(big) :]
        smalls, refs = refs[: len(small)], refs[len(small) :]
        outs, refs = refs[: len(out_shape)], refs[len(out_shape) :]
        scratches, done = refs[: len(scratch)], refs[-1]
        index, own = place_ref[0], place_ref[1]
        started, used = [], 0
        for sources, *_, which in groups:
            for source, block in zip(sources, which):
                whole, root = scratches[2 * len(started)], scratches[2 * len(started) + 1]
                mine = []
                if len(source.arrays) == 1:
                    ref = bigs[place[id(source.arrays[0])]]
                    mine.append((ref.at[:, pl.ds(source.start, source.columns)], whole.at[0]))
                else:
                    deep = source.arrays[0].shape[0] // befores
                    half = source.arrays[0].shape[2]
                    for part in range(4):
                        ref = bigs[place[id(source.arrays[part])]]
                        core = own if part < 2 else 1 - own
                        for before in range(befores):
                            from_ref = ref.at[
                                pl.ds(before * deep, deep), pl.ds(source.start, source.height)
                            ]
                            to_ref = whole.at[
                                pl.ds((2 * before + core) * deep, deep),
                                :,
                                pl.ds((part % 2) * half, half),
                            ]
                            mine.append((from_ref, to_ref))
                mine.append((bigs[0].at[:, pl.ds(block * side, side)], root))
                group = []
                for from_ref, to_ref in mine:
                    copy = pltpu.make_async_copy(from_ref, to_ref, done.at[used])
                    copy.start()
                    group.append(copy)
                    used += 1
                started.append(group)
        matrix = 0
        for i, (sources, _, left_stats, right_stats, _, weights, _) in enumerate(groups):
            rows, columns = left_stats.shape[2], right_stats.shape[2]
            high, wide = left_stats.shape[1], right_stats.shape[1]
            shard_ref, left_ref, right_ref, root_ref = smalls[:4]
            weight_ref = None if weights is None else smalls[4]
            smalls = smalls[4 if weights is None else 5 :]
            left_out, right_out, third_out = outs[3 * i : 3 * i + 3]
            lane = lax.broadcasted_iota(jnp.int32, (wide, columns), 1)
            row = lax.broadcasted_iota(jnp.int32, (wide, columns), 0)
            pick = (lane == row + index * wide).astype(F32)
            for j in range(len(sources)):
                for copy in started[matrix]:
                    copy.wait()
                whole = scratches[2 * matrix][...].reshape(rows, columns)
                other = scratches[2 * matrix + 1][...]
                matrix += 1
                stacked = [shard_ref[j], pick] + ([root_ref[j]] if weights is None else [])
                first = against(jnp.concatenate(stacked, axis=0).astype(BF16), whole)
                left_out[j] = 0.5 * left_ref[j] + (0.5 / columns) * first[:high]
                picked = first[high : high + wide]
                if weights is None:
                    second = product(picked.astype(BF16), whole)
                    right_out[j] = 0.5 * right_ref[j] + (0.5 / rows) * second
                    turned = first[high + wide :].astype(BF16)
                    third_out[j] = product(turned, other).astype(BF16)
                else:
                    stacked = jnp.concatenate([root_ref[j], picked], axis=0).astype(BF16)
                    second = product(stacked, whole)
                    right_out[j] = 0.5 * right_ref[j] + (0.5 / rows) * second[high:]
                    step = product(second[:high].astype(BF16), other)
                    third_out[j] = weight_ref[j] - step * (1.0 / math.sqrt(rows))

    vmem = pl.BlockSpec(memory_space=pltpu.VMEM)
    results = pl.pallas_call(
        kernel,
        out_shape=out_shape,
        in_specs=[pl.BlockSpec(memory_space=pltpu.SMEM)]
        + [pl.BlockSpec(memory_space=pl.ANY)] * len(big)
        + [vmem] * len(small),
        out_specs=[vmem] * len(out_shape),
        scratch_shapes=scratch + [pltpu.SemaphoreType.DMA((copies,))],
        compiler_params=pltpu.CompilerParams(vmem_limit_bytes=56 << 20),
    )(bits, *big, *small)
    return [results[3 * i : 3 * i + 3] for i in range(len(groups))]


def body(
    embedding,
    latent,
    segment_ids,
    cotangent,
    weight_adapt,
    weight_attn,
    weight_gateup,
    weight_down,
    norm_gains,
    left_adapt,
    right_adapt,
    left_attn,
    right_attn,
    left_gateup,
    right_gateup,
    left_down,
    right_down,
    left_root_adapt,
    right_root_adapt,
    left_root_attn,
    right_root_attn,
    left_root_gateup,
    right_root_gateup,
    left_root_down,
    right_root_down,
    gain_moment,
):
    n_dp, n_seq = lax.axis_size("dp"), lax.axis_size("seq")
    links = Links(n_dp, n_seq)
    seq_count, group_len, width = embedding.shape
    tokens = seq_count * group_len
    length = group_len * n_seq
    hidden_width = weight_gateup.shape[2]
    by_heads = HEADS % n_seq == 0

    gain_share = norm_gains.shape[1]
    small = jnp.concatenate(
        [norm_gains.astype(BF16).reshape(-1), segment_ids.astype(BF16).reshape(-1)]
    )
    small = jnp.pad(small[None], ((0, 7), (0, width - small.shape[0])))
    attn_rows = weight_attn.astype(BF16)
    first = Gathering(links, [weight_adapt.astype(BF16), small])
    second = Gathering(links, [attn_rows[i] for i in range(4)])
    third = Gathering(links, [weight_down.astype(BF16)])
    gateup_rows = weight_gateup.astype(BF16)
    gateup_rows = jnp.concatenate([gateup_rows[0], gateup_rows[1]], axis=1)
    inner_steps, cross_steps = range(len(links.inner)), range(links.steps)
    for step in inner_steps:
        first.inside(step)
    (gateup_rows,) = tick([first, second], gateup_rows)
    gateup_full = lax.all_gather(gateup_rows, AXES, axis=0, tiled=True)
    for step in inner_steps:
        second.inside(step)
    for step in cross_steps:
        first.cross(step)
    tick([first, second, third])
    first.core()
    adapt_full, small = first.finish()
    for step in cross_steps:
        second.cross(step)
    for step in inner_steps:
        third.inside(step)
    tick([second, third])
    second.core()
    query_full, key_full, value_full, out_full = second.finish()
    for step in cross_steps:
        third.cross(step)
    third.core()
    (down_full,) = third.finish()

    small = small.reshape(links.count, 8, width)[:, 0]
    gain_values = small[:, : 4 * gain_share].reshape(links.count, 4, gain_share)
    gain_values = gain_values.transpose(1, 0, 2).reshape(4, width).astype(F32)
    ids = small[:, 4 * gain_share : 4 * gain_share + tokens].reshape(n_dp, n_seq, seq_count, -1)
    ids = lax.dynamic_index_in_dim(ids, lax.axis_index("dp"), 0, False)
    segment_whole = ids.transpose(1, 0, 2).reshape(seq_count, length).astype(jnp.int32)

    all_places = jnp.arange(length, dtype=jnp.int32)
    doc_starts = jnp.sum(
        (segment_whole[:, None, :] < segment_whole[:, :, None]).astype(jnp.int32), axis=2
    )
    places = all_places[None, :] - doc_starts
    half_dim = HEAD_DIM // 2
    frequency = THETA ** (-jnp.arange(half_dim, dtype=F32) / half_dim)
    angles = places.astype(F32)[..., None] * frequency
    cosine_all, sine_all = jnp.cos(angles), jnp.sin(angles)
    own_start = links.seq_index * group_len
    cosine = lax.dynamic_slice_in_dim(cosine_all, own_start, group_len, 1)
    sine_table = lax.dynamic_slice_in_dim(sine_all, own_start, group_len, 1)
    if by_heads:
        query_places, segment_query = all_places, segment_whole
        cosine_back, sine_back = cosine_all[:, None], sine_all[:, None]
    else:
        query_places, segment_query = own_start + jnp.arange(group_len), segment_ids
        cosine_back, sine_back = cosine[:, None], sine_table[:, None]
    allowed = (all_places[None, None, :] <= query_places[None, :, None]) & (
        segment_whole[:, None, :] == segment_query[:, :, None]
    )

    def to_heads(values):
        parts = values.shape[2]
        values = values.transpose(3, 2, 0, 1, 4)
        came = lax.all_to_all(values, "seq", 0, 0, tiled=True)
        came = came.reshape(n_seq, HEADS // n_seq, parts, seq_count, group_len, HEAD_DIM)
        came = came.transpose(2, 3, 1, 0, 4, 5)
        return came.reshape(parts, seq_count, HEADS // n_seq, length, HEAD_DIM)

    def to_tokens(values):
        parts = values.shape[0]
        own = HEADS // n_seq
        values = values.reshape(parts, seq_count, own, n_seq, group_len, HEAD_DIM)
        values = values.transpose(3, 2, 0, 1, 4, 5)
        came = lax.all_to_all(values, "seq", 0, 0, tiled=True)
        came = came.reshape(HEADS, parts, seq_count, group_len, HEAD_DIM)
        return came.transpose(1, 2, 3, 0, 4)

    scaling = 1.0 / math.sqrt(HEAD_DIM)

    def attention(queries, keys, values):
        if by_heads:
            queries, keys, values = to_heads(jnp.stack([queries, keys, values], axis=2))
        else:
            queries = queries.transpose(0, 2, 1, 3)
            keys, values = (
                lax.all_gather(item, "seq", axis=1, tiled=True).transpose(0, 2, 1, 3)
                for item in (keys, values)
            )
        scores = jnp.einsum("shqd,shkd->shqk", queries, keys, preferred_element_type=F32)
        scores = jnp.where(allowed[:, None], scores * scaling, -1e30)
        exponent = jnp.exp(scores - jnp.max(scores, axis=-1, keepdims=True))
        soft_full = exponent / jnp.sum(exponent, axis=-1, keepdims=True)
        mixed = jnp.einsum(
            "shqk,shkd->shqd", soft_full.astype(BF16), values, preferred_element_type=F32
        ).astype(BF16)
        if by_heads:
            mixed = to_tokens(mixed[None])[0]
        else:
            mixed = mixed.transpose(0, 2, 1, 3)
        return mixed.reshape(tokens, width), (queries, keys, values, soft_full)

    def attention_back(mixed_grad, saved):
        queries, keys, values, soft_full = saved
        soft_grad = jnp.einsum("shqd,shkd->shqk", mixed_grad, values, preferred_element_type=F32)
        inner_sum = jnp.sum(soft_full * soft_grad, axis=-1, keepdims=True)
        score_grad = (soft_full * (soft_grad - inner_sum)).astype(BF16)
        query_grad = (
            jnp.einsum("shqk,shkd->shqd", score_grad, keys, preferred_element_type=F32) * scaling
        )
        key_grad = (
            jnp.einsum("shqk,shqd->shkd", score_grad, queries, preferred_element_type=F32)
            * scaling
        )
        value_grad = jnp.einsum(
            "shqk,shqd->shkd", soft_full.astype(BF16), mixed_grad, preferred_element_type=F32
        )
        if by_heads:
            query_grad = rotate(query_grad, cosine_back, -sine_back).astype(BF16)
            key_grad = rotate(key_grad, cosine_back, -sine_back).astype(BF16)
            value_grad = value_grad.astype(BF16)
            return jnp.stack([query_grad, key_grad, value_grad])
        key_grad, value_grad = (
            lax.psum_scatter(item.astype(BF16), "seq", scatter_dimension=2, tiled=True).astype(F32)
            for item in (key_grad, value_grad)
        )
        query_grad = rotate(query_grad, cosine_back, -sine_back).astype(BF16)
        key_grad = rotate(key_grad, cosine_back, -sine_back).astype(BF16)
        grads = jnp.stack([query_grad, key_grad, value_grad.astype(BF16)])
        return grads.transpose(0, 1, 3, 2, 4)

    embed_flat = embedding.reshape(tokens, width)
    embed_part = product(embed_flat, adapt_full[width:])
    root_stack = jnp.concatenate(
        [
            right_root_adapt.astype(BF16)[:, None],
            right_root_attn.astype(BF16).transpose(1, 0, 2),
            right_root_down.astype(BF16)[:, None],
            left_root_gateup.astype(BF16).transpose(1, 0, 2),
        ],
        axis=1,
    )
    root_stack = root_stack.reshape(root_stack.shape[0], 8 * width)
    roots = []

    def forward(latent_low):
        start_sum = product(latent_low, adapt_full[:width]) + embed_part
        scale_one = norm_scale(start_sum)
        normed_one = (start_sum * scale_one * gain_values[0]).astype(BF16)
        head_shape = (seq_count, group_len, HEADS, HEAD_DIM)
        turn_cos, turn_sin = cosine[:, :, None, :], sine_table[:, :, None, :]
        queries = product(normed_one, query_full).reshape(head_shape)
        queries = rotate(queries, turn_cos, turn_sin).astype(BF16)
        keys = product(normed_one, key_full).reshape(head_shape)
        keys = rotate(keys, turn_cos, turn_sin).astype(BF16)
        values = product(normed_one, value_full).astype(BF16).reshape(head_shape)
        tied = len(roots) > 0
        if not tied:
            tied_stack, queries = tie(root_stack, queries)
            roots.append(lax.all_gather(tied_stack, AXES, axis=0, tiled=True))
        mixed_heads, attended = attention(queries, keys, values)
        if tied:
            roots[0], mixed_heads = tie(roots[0], mixed_heads)
        branch = product(mixed_heads, out_full)
        scale_two = norm_scale(branch)
        middle = start_sum + branch * scale_two * gain_values[1]
        scale_three = norm_scale(middle)
        normed_three = (middle * scale_three * gain_values[2]).astype(BF16)
        both = product(normed_three, gateup_full)
        gate_value, upward = both[:, :hidden_width], both[:, hidden_width:]
        hidden = (jax.nn.silu(gate_value) * upward).astype(BF16)
        feed_out = product(hidden, down_full)
        scale_four = norm_scale(feed_out)
        result = middle + feed_out * scale_four * gain_values[3]
        saved_values = (
            start_sum,
            scale_one,
            normed_one,
            attended,
            mixed_heads,
            branch,
            scale_two,
            middle,
            scale_three,
            normed_three,
            gate_value,
            upward,
            hidden,
            feed_out,
            scale_four,
        )
        return (result, saved_values)

    latent_low = latent.reshape(tokens, width)
    latent_state, unused_saved = forward(latent_low)
    latent_low = latent_state.astype(BF16)
    final_state, saved_values = forward(latent_low)
    (
        start_sum,
        scale_one,
        normed_one,
        attended,
        mixed_heads,
        branch,
        scale_two,
        middle,
        scale_three,
        normed_three,
        gate_value,
        upward,
        hidden,
        feed_out,
        scale_four,
    ) = saved_values
    factor = 1.0 / math.sqrt(seq_count * n_dp * length)
    incoming = cotangent.astype(F32).reshape(tokens, width)
    feed_grad, gain_four = norm_back(feed_out, scale_four, gain_values[3], incoming)
    feed_grad = feed_grad.astype(BF16)
    down_sum = Reduction(links, width)
    down_sum.send(hidden, feed_grad)
    hidden_grad = against(feed_grad, down_full)
    gate_grad = (hidden_grad * upward * silu_grad(gate_value)).astype(BF16)
    up_grad = (hidden_grad * jax.nn.silu(gate_value)).astype(BF16)
    gateup_sum = Reduction(links, hidden_width)
    gateup_sum.send(normed_three, gate_grad)
    gateup_sum.send(normed_three, up_grad)
    both_grad = jnp.concatenate([gate_grad, up_grad], axis=1)
    normed_three_grad = against(both_grad, gateup_full)
    middle_grad, gain_three = norm_back(middle, scale_three, gain_values[2], normed_three_grad)
    middle_grad = middle_grad + incoming
    branch_grad, gain_two = norm_back(branch, scale_two, gain_values[1], middle_grad)
    branch_grad = branch_grad.astype(BF16)
    mixed_grad = against(branch_grad, out_full).astype(BF16)
    rest_sum = Reduction(links, width)
    rest_sum.send(mixed_heads, branch_grad)
    down_sum.add()
    (mixed_grad,) = tick([down_sum], mixed_grad)
    mixed_grad = mixed_grad.reshape(seq_count, group_len, HEADS, HEAD_DIM)
    if by_heads:
        mixed_grad = to_heads(mixed_grad[:, :, None])[0]
    else:
        mixed_grad = mixed_grad.transpose(0, 2, 1, 3)
    down_sum.cross(0)
    gateup_sum.add()
    gateup_sum.cross(0)
    (mixed_grad,) = tick([down_sum], mixed_grad)
    grads = attention_back(mixed_grad, attended)
    for step in cross_steps[1:]:
        down_sum.cross(step)
        gateup_sum.cross(step)
    if by_heads:
        grads = to_tokens(grads)
    query_pre, key_pre, value_pre = grads.reshape(3, tokens, width)
    query_pre, key_pre, value_pre = tick([down_sum], query_pre, key_pre, value_pre)
    rest_sum.send(normed_one, jnp.concatenate([query_pre, key_pre, value_pre], axis=1))
    normed_one_grad = (
        against(query_pre, query_full) + against(key_pre, key_full) + against(value_pre, value_full)
    )
    start_grad, gain_one = norm_back(start_sum, scale_one, gain_values[0], normed_one_grad)
    start_grad = (start_grad + middle_grad).astype(BF16)
    joined = jnp.concatenate([latent_low, embed_flat], axis=1)
    rest_sum.send(joined, start_grad)
    gain_sums = jnp.stack([gain_one, gain_two, gain_three, gain_four])
    gain_sums = gain_sums.reshape(4, links.count, gain_share).transpose(1, 0, 2)
    gain_sums = gain_sums.reshape(links.count, 1, 4 * gain_share)
    gain_sums = jnp.pad(gain_sums, ((0, 0), (0, 7), (0, width - 4 * gain_share)))
    rest_sum.send_rows(gain_sums.reshape(-1, width))
    rest_sum.add()
    root_rows = roots[0]
    (start_grad,) = tick([gateup_sum, down_sum, rest_sum], start_grad)
    rest_sum.cross(0)
    for step in inner_steps:
        gateup_sum.inside(step)
    tick([rest_sum, gateup_sum])
    gate_shards = (gateup_sum.parts[0] * factor).reshape(2, -1, hidden_width)
    full_both = lax.all_gather(
        jnp.concatenate([gate_shards[0], gate_shards[1]], axis=1).astype(BF16),
        AXES,
        axis=0,
        tiled=True,
    )
    for step in cross_steps[1:]:
        rest_sum.cross(step)
    for step in inner_steps:
        down_sum.inside(step)
    tick([rest_sum, down_sum])
    reduced_down = down_sum.parts[0] * factor
    first = Gathering(links, [reduced_down.astype(BF16)])
    left_root_adapt, left_root_attn, left_root_down, right_root_gateup, reduced_down = tie(
        left_root_adapt, left_root_attn, left_root_down, right_root_gateup, reduced_down
    )
    rest_sum.inside(0)
    first.inside(0)
    tick([rest_sum, first])
    for step in inner_steps[1:]:
        rest_sum.inside(step)
        first.inside(step)
    tick([rest_sum, first])
    reduced_rest = rest_sum.parts[0] * factor
    row_share = width // links.count
    attn_shards = reduced_rest[: 4 * row_share].reshape(4, row_share, width)
    attn_shards = jnp.concatenate([attn_shards[1:], attn_shards[:1]], axis=0)
    reduced_adapt = reduced_rest[4 * row_share : 6 * row_share]
    reduced_gains = reduced_rest[6 * row_share, : 4 * gain_share].reshape(4, gain_share)
    third = Gathering(
        links, [attn_shards[i].astype(BF16) for i in range(4)] + [reduced_adapt.astype(BF16)]
    )
    third.inside(0)
    first.cross(0)
    (full_both,) = tick([third, first], full_both)
    def statistics(shard, whole, left_stat, right_stat, left_root):
        rows, columns = whole.shape
        new_left = 0.5 * left_stat + (0.5 / columns) * against(shard.astype(BF16), whole)
        count = right_stat.shape[0]
        own = lax.dynamic_slice_in_dim(whole, links.index * count, count, 1).T
        if left_root is None:
            return (new_left, 0.5 * right_stat + (0.5 / rows) * product(own, whole), None)
        own_count = left_root.shape[0]
        both = product(jnp.concatenate([left_root.astype(BF16), own], axis=0), whole)
        return (new_left, 0.5 * right_stat + (0.5 / rows) * both[own_count:], both[:own_count])

    def whole_step(part, which, rows):
        root = root_rows[:, which * width : (which + 1) * width]
        return product(part.astype(BF16), root) * (1.0 / math.sqrt(rows))

    for step in inner_steps[1:]:
        third.inside(step)
    for step in cross_steps[1:]:
        first.cross(step)
    fits = row_share % 16 == 0
    if fits:
        sources = [Source([full_both], i * hidden_width, width, hidden_width) for i in range(2)]
        ((new_left_gateup, new_right_gateup, step_columns),) = shampoo(
            links,
            [
                (
                    sources,
                    gate_shards,
                    left_gateup,
                    right_gateup,
                    right_root_gateup,
                    None,
                    [6, 7],
                )
            ],
            root_rows,
        )
        step_columns = step_columns.transpose(0, 2, 1)
    else:
        whole_gates = [full_both[:, :hidden_width], full_both[:, hidden_width:]]
        gateup_parts = [
            statistics(gate_shards[i], whole_gates[i], left_gateup[i], right_gateup[i], None)
            for i in range(2)
        ]
        step_columns = []
        for i in range(2):
            turned = against(whole_gates[i], right_root_gateup[i].astype(BF16)).astype(BF16)
            root = root_rows[:, (6 + i) * width : (7 + i) * width]
            step_columns.append(product(root, turned).astype(BF16))
        step_columns = jnp.stack(step_columns)
        new_left_gateup = jnp.stack([member[0] for member in gateup_parts])
        new_right_gateup = jnp.stack([member[1] for member in gateup_parts])
    ff_share = step_columns.shape[2]
    step_columns = step_columns.reshape(2, links.count, row_share, ff_share).transpose(1, 0, 2, 3)
    (step_columns,) = tick([third, first], step_columns)
    first.core()
    step_rows = lax.all_to_all(step_columns, AXES, 0, 0, tiled=True)
    step_gateup = step_rows.transpose(1, 2, 0, 3).reshape(2, row_share, hidden_width)
    new_gateup = weight_gateup - step_gateup.astype(F32) * (1.0 / math.sqrt(width))

    third.cross(0)
    (new_gateup,) = tick([third, first], new_gateup)
    for step in cross_steps[1:]:
        third.cross(step)
    if fits:
        down_group = (
            first.sources(),
            reduced_down[None],
            left_down[None],
            right_down[None],
            left_root_down[None],
            weight_down[None],
            [5],
        )
        ((new_left_down, new_right_down, new_down),) = shampoo(links, [down_group], root_rows)
        new_left_down, new_right_down, new_down = new_left_down[0], new_right_down[0], new_down[0]
    else:
        (full_down,) = first.finish()
        new_left_down, new_right_down, down_part = statistics(
            reduced_down, full_down, left_down, right_down, left_root_down
        )
        new_down = weight_down - whole_step(down_part, 5, hidden_width)
    (new_down,) = tick([third], new_down)
    third.core()
    tick([third])
    grad_embedding = against(start_grad, adapt_full[width:]).reshape(
        seq_count, group_len, width
    )
    if fits:
        sources = third.sources()
        attn_group = (
            sources[:4],
            attn_shards,
            left_attn,
            right_attn,
            left_root_attn,
            weight_attn,
            [1, 2, 3, 4],
        )
        adapt_group = (
            sources[4:],
            reduced_adapt[None],
            left_adapt[None],
            right_adapt[None],
            left_root_adapt[None],
            weight_adapt[None],
            [0],
        )
        (
            (new_left_attn, new_right_attn, new_attn),
            (new_left_adapt, new_right_adapt, new_adapt),
        ) = shampoo(links, [attn_group, adapt_group], root_rows)
        new_left_adapt, new_right_adapt, new_adapt = (
            new_left_adapt[0],
            new_right_adapt[0],
            new_adapt[0],
        )
    else:
        *attn_wholes, full_adapt = third.finish()
        attn_parts = [
            statistics(
                attn_shards[i], attn_wholes[i], left_attn[i], right_attn[i], left_root_attn[i]
            )
            for i in range(4)
        ]
        new_attn = weight_attn - jnp.stack(
            [whole_step(attn_parts[i][2], 1 + i, width) for i in range(4)]
        )
        new_left_attn = jnp.stack([member[0] for member in attn_parts])
        new_right_attn = jnp.stack([member[1] for member in attn_parts])
        new_left_adapt, new_right_adapt, adapt_part = statistics(
            reduced_adapt, full_adapt, left_adapt, right_adapt, left_root_adapt
        )
        new_adapt = weight_adapt - whole_step(adapt_part, 0, 2 * width)
    new_gain_moment = 0.5 * gain_moment + 0.5 * reduced_gains * reduced_gains
    new_norm_gains = norm_gains - 0.5 * reduced_gains / (jnp.sqrt(new_gain_moment) + 1e-08)
    latent_out = final_state.reshape(seq_count, group_len, width).astype(BF16)
    return (
        latent_out,
        grad_embedding,
        reduced_adapt,
        attn_shards,
        gate_shards,
        reduced_down,
        reduced_gains,
        new_left_adapt,
        new_right_adapt,
        new_left_attn,
        new_right_attn,
        new_left_gateup,
        new_right_gateup,
        new_left_down,
        new_right_down,
        new_adapt,
        new_attn,
        new_gateup,
        new_down,
        new_gain_moment,
        new_norm_gains,
    )

def solution(mesh):
    return jax.shard_map(
        body,
        mesh=mesh,
        in_specs=(
            P("dp", "seq", None),
            P("dp", "seq", None),
            P("dp", "seq"),
            P("dp", "seq", None),
            P(("dp", "seq"), None),
            P(None, ("dp", "seq"), None),
            P(None, ("dp", "seq"), None),
            P(("dp", "seq"), None),
            P(None, ("dp", "seq")),
            P(("dp", "seq"), None),
            P(("dp", "seq"), None),
            P(None, ("dp", "seq"), None),
            P(None, ("dp", "seq"), None),
            P(None, ("dp", "seq"), None),
            P(None, ("dp", "seq"), None),
            P(("dp", "seq"), None),
            P(("dp", "seq"), None),
            P(("dp", "seq"), None),
            P(("dp", "seq"), None),
            P(None, ("dp", "seq"), None),
            P(None, ("dp", "seq"), None),
            P(None, ("dp", "seq"), None),
            P(None, ("dp", "seq"), None),
            P(("dp", "seq"), None),
            P(("dp", "seq"), None),
            P(None, ("dp", "seq")),
        ),
        out_specs=(
            P("dp", "seq", None),
            P("dp", "seq", None),
            P(("dp", "seq"), None),
            P(None, ("dp", "seq"), None),
            P(None, ("dp", "seq"), None),
            P(("dp", "seq"), None),
            P(None, ("dp", "seq")),
            P(("dp", "seq"), None),
            P(("dp", "seq"), None),
            P(None, ("dp", "seq"), None),
            P(None, ("dp", "seq"), None),
            P(None, ("dp", "seq"), None),
            P(None, ("dp", "seq"), None),
            P(("dp", "seq"), None),
            P(("dp", "seq"), None),
            P(("dp", "seq"), None),
            P(None, ("dp", "seq"), None),
            P(None, ("dp", "seq"), None),
            P(("dp", "seq"), None),
            P(None, ("dp", "seq")),
            P(None, ("dp", "seq")),
        ),
        check_vma=False,
    )
```

```python
import math

import jax
import jax.numpy as jnp
from jax import lax
from jax.experimental import pallas as pl
from jax.experimental.pallas import tpu as pltpu
from jax.sharding import PartitionSpec as P

HEADS = 8
HEAD_DIM = 128
EPSILON = 1e-06
THETA = 50000.0
AXES = ("dp", "seq")
BF16 = jnp.bfloat16
F32 = jnp.float32


def product(left_side, right_side):
    return jnp.dot(left_side, right_side, preferred_element_type=F32)


def across(left_side, right_side):
    return lax.dot_general(
        left_side, right_side, (((0,), (0,)), ((), ())), preferred_element_type=F32
    )


def against(left_side, right_side):
    return lax.dot_general(
        left_side, right_side, (((1,), (1,)), ((), ())), preferred_element_type=F32
    )


def norm_scale(values):
    return lax.rsqrt(jnp.mean(values * values, axis=-1, keepdims=True) + EPSILON)


def norm_back(values, scaling, gain_row, gradient):
    unit_rows = values * scaling
    weighted = gradient * gain_row
    moved = scaling * (
        weighted - unit_rows * jnp.mean(unit_rows * weighted, axis=-1, keepdims=True)
    )
    return (moved, jnp.sum(gradient * unit_rows, axis=0))


def rotate(values, cosine, sine_table):
    half_dim = values.shape[-1] // 2
    first_half = values[..., :half_dim]
    second_half = values[..., half_dim:]
    return jnp.concatenate(
        [
            first_half * cosine - second_half * sine_table,
            second_half * cosine + first_half * sine_table,
        ],
        axis=-1,
    )


def silu_grad(values):
    sigmoid_value = jax.nn.sigmoid(values)
    return sigmoid_value * (1.0 + values * (1.0 - sigmoid_value))


def tie(*values):
    return lax.optimization_barrier(values)


def tick(works, *values):
    flat = [part for work in works for part in work.parts]
    tied = list(lax.optimization_barrier(tuple(flat) + values))
    for work in works:
        count = len(work.parts)
        work.parts, tied = tied[:count], tied[count:]
    return tied


class Links:
    def __init__(self, n_dp, n_seq):
        self.count = n_dp * n_seq
        self.bits = (self.count - 1).bit_length()
        self.core = (n_dp - 1).bit_length() - 1
        self.last = self.bits - 1
        self.upper = list(range(self.core))
        self.inner = list(range(self.core + 1, self.last))
        self.index = lax.axis_index("dp") * n_seq + lax.axis_index("seq")
        self.seq_index = lax.axis_index("seq")
        self.pairs = [
            [(i, i ^ (1 << (self.bits - 1 - bit))) for i in range(self.count)]
            for bit in range(self.bits)
        ]
        self.steps = len(self.upper) + 1

    def own(self, bit):
        return (self.index >> (self.bits - 1 - bit)) & 1

    def swap(self, values, bit):
        return lax.ppermute(values, AXES, self.pairs[bit])


class Gathering:
    def __init__(self, links, shards):
        self.links = links
        self.heights = [shard.shape[0] for shard in shards]
        self.rows = sum(self.heights)
        shard = shards[0] if len(shards) == 1 else jnp.concatenate(shards, axis=0)
        self.parts = [shard]
        self.known = [[]]

    def widen(self, i, bit):
        links, part, known = self.links, self.parts[i], self.known[i]
        came = links.swap(part, bit)
        columns = part.shape[1]
        before = 1 << sum(1 for other in known if other < bit)
        mine = part.reshape(before, 1, -1, columns)
        both = jnp.zeros((before, 2) + mine.shape[2:], part.dtype)
        both = lax.dynamic_update_slice(both, mine, (0, links.own(bit), 0, 0))
        both = lax.dynamic_update_slice(
            both, came.reshape(mine.shape), (0, 1 - links.own(bit), 0, 0)
        )
        self.parts[i] = both.reshape(-1, columns)
        self.known[i] = known + [bit]

    def inside(self, step):
        self.widen(0, self.links.inner[step])

    def cross(self, step):
        links = self.links
        if len(self.parts) == 1:
            half = self.parts[0].shape[1] // 2
            self.parts = [self.parts[0][:, :half], self.parts[0][:, half:]]
            self.known = [self.known[0], self.known[0]]
        orders = ([links.last] + links.upper, links.upper + [links.last])
        for i in range(2):
            self.widen(i, orders[i][step])

    def core(self):
        self.parts += [self.links.swap(part, self.links.core) for part in self.parts]

    def finish(self):
        links = self.links
        before, half = 1 << len(links.upper), self.parts[0].shape[1]
        four = [part.reshape(before, -1, self.rows, half) for part in self.parts]
        wholes, row = [], 0
        for height in self.heights:
            piece = [part[:, :, row : row + height] for part in four]
            own = links.own(links.core)
            whole = jnp.zeros((before, 2) + piece[0].shape[1:3] + (2 * half,), piece[0].dtype)
            for i in range(4):
                place = own if i < 2 else 1 - own
                whole = lax.dynamic_update_slice(
                    whole, piece[i][:, None], (0, place, 0, 0, (i % 2) * half)
                )
            wholes.append(whole.reshape(-1, 2 * half))
            row += height
        return wholes

    def sources(self):
        columns = 2 * self.parts[0].shape[1]
        befores = 1 << len(self.links.upper)
        if len(self.heights) == 1:
            arrays = [part.reshape(befores, -1, part.shape[1]) for part in self.parts]
            return [Source(arrays, 0, arrays[0].shape[1], columns)]
        arrays = [part.reshape(-1, self.rows, part.shape[1]) for part in self.parts]
        sources, row = [], 0
        for height in self.heights:
            sources.append(Source(arrays, row, height, columns))
            row += height
        return sources


class Reduction:
    def __init__(self, links, wide):
        self.links, self.wide = links, wide
        self.terms = []

    def sides(self, left_side, which):
        blocks = 2 << len(self.links.upper)
        wide = left_side.shape[1] // blocks
        chosen = []
        for block in range(0, blocks, 2):
            first = left_side[:, block * wide : (block + 1) * wide]
            second = left_side[:, (block + 1) * wide : (block + 2) * wide]
            chosen.append(jnp.where(which == 0, first, second))
        return jnp.concatenate(chosen, axis=1)

    def early(self, left_side):
        links = self.links
        away = self.sides(left_side, 1 - links.own(links.core))
        kept = self.sides(left_side, links.own(links.core))
        return (kept, links.swap(away, links.core))

    def send(self, left_pair, right_side):
        other = self.links.swap(right_side, self.links.core)
        left_both = jnp.concatenate(left_pair, axis=0)
        self.terms.append(lambda: across(left_both, jnp.concatenate([right_side, other], axis=0)))

    def send_rows(self, values):
        links = self.links
        halves = values.reshape(1 << len(links.upper), 2, -1, values.shape[1])
        own = links.own(links.core)
        away = lax.dynamic_index_in_dim(halves, 1 - own, 1, False).reshape(-1, values.shape[1])
        kept = lax.dynamic_index_in_dim(halves, own, 1, False).reshape(-1, values.shape[1])
        came = links.swap(away.astype(BF16), links.core)
        self.terms.append(lambda: kept + came.astype(F32))

    def add(self):
        links = self.links
        owners = links.count // 2
        total = []
        for term in self.terms:
            item = term().astype(BF16)
            item = item.reshape(owners, -1, item.shape[1])
            for start in range(0, item.shape[2], self.wide):
                total.append(item[:, :, start : start + self.wide])
        total = total[0] if len(total) == 1 else jnp.concatenate(total, axis=1)
        total = total.reshape(-1, total.shape[2])
        half = total.shape[1] // 2
        self.parts = [total[:, :half], total[:, half:]]
        left = [bit for bit in range(links.bits) if bit != links.core]
        self.left = [list(left), list(left)]

    def halve(self, i, bit, out_type=BF16):
        links, part = self.links, self.parts[i]
        columns = part.shape[1]
        before = 1 << sum(1 for other in self.left[i] if other < bit)
        both = part.reshape(before, 2, -1, columns)
        own = links.own(bit)
        away = lax.dynamic_index_in_dim(both, 1 - own, 1, False)
        kept = lax.dynamic_index_in_dim(both, own, 1, False)
        came = links.swap(away.reshape(-1, columns), bit)
        kept = kept.reshape(-1, columns).astype(F32) + came.astype(F32)
        self.parts[i] = kept.astype(out_type)
        self.left[i].remove(bit)

    def cross(self, step):
        links = self.links
        orders = (links.upper + [links.last], [links.last] + links.upper)
        for i in range(2):
            self.halve(i, orders[i][step])

    def join(self, other):
        owners = 1 << len(self.left[0])
        for i in range(2):
            both = [part.reshape(owners, -1, part.shape[1]) for part in (self.parts[i], other.parts[i])]
            self.parts[i] = jnp.concatenate(both, axis=1).reshape(-1, both[0].shape[2])

    def inside(self, step):
        if len(self.parts) == 2:
            self.parts = [jnp.concatenate(self.parts, axis=1)]
        final = step == len(self.links.inner) - 1
        self.halve(0, self.links.inner[-1 - step], F32 if final else BF16)


class Source:
    def __init__(self, arrays, start, height, columns):
        self.arrays, self.start, self.height, self.columns = arrays, start, height, columns


def shampoo(links, groups, roots):
    side = roots.shape[0]
    befores = 1 << len(links.upper)
    big = [roots]
    for sources, *_ in groups:
        for source in sources:
            for array in source.arrays:
                if not any(array is other for other in big):
                    big.append(array)
    place = {id(array): i for i, array in enumerate(big)}
    small, out_shape, scratch, copies = [], [], [], 0
    for sources, shards, left_stats, right_stats, own_roots, weights, which in groups:
        count, _, rows = left_stats.shape
        columns = right_stats.shape[2]
        small += [shards, left_stats, right_stats, own_roots]
        small += [] if weights is None else [weights]
        third = (count, right_stats.shape[1], rows) if weights is None else weights.shape
        out_shape += [
            jax.ShapeDtypeStruct(left_stats.shape, F32),
            jax.ShapeDtypeStruct(right_stats.shape, F32),
            jax.ShapeDtypeStruct(third, BF16 if weights is None else F32),
        ]
        for source in sources:
            if len(source.arrays) == 1:
                scratch.append(pltpu.VMEM((1, rows, columns), BF16))
                copies += 2
            else:
                blocks = 2 * source.arrays[0].shape[0]
                scratch.append(pltpu.VMEM((blocks, rows // blocks, columns), BF16))
                copies += 4 * befores + 1
            scratch.append(pltpu.VMEM((side, side), BF16))
    bits = jnp.stack([links.index, links.own(links.core)]).astype(jnp.int32)

    def kernel(*refs):
        place_ref, refs = refs[0], list(refs[1:])
        bigs, refs = refs[: len(big)], refs[len(big) :]
        smalls, refs = refs[: len(small)], refs[len(small) :]
        outs, refs = refs[: len(out_shape)], refs[len(out_shape) :]
        scratches, done = refs[: len(scratch)], refs[-1]
        index, own = place_ref[0], place_ref[1]
        started, used = [], 0
        for sources, *_, which in groups:
            for source, block in zip(sources, which):
                whole, root = scratches[2 * len(started)], scratches[2 * len(started) + 1]
                mine = []
                if len(source.arrays) == 1:
                    ref = bigs[place[id(source.arrays[0])]]
                    mine.append((ref.at[:, pl.ds(source.start, source.columns)], whole.at[0]))
                else:
                    deep = source.arrays[0].shape[0] // befores
                    half = source.arrays[0].shape[2]
                    for part in range(4):
                        ref = bigs[place[id(source.arrays[part])]]
                        core = own if part < 2 else 1 - own
                        for before in range(befores):
                            from_ref = ref.at[
                                pl.ds(before * deep, deep), pl.ds(source.start, source.height)
                            ]
                            to_ref = whole.at[
                                pl.ds((2 * before + core) * deep, deep),
                                :,
                                pl.ds((part % 2) * half, half),
                            ]
                            mine.append((from_ref, to_ref))
                mine.append((bigs[0].at[:, pl.ds(block * side, side)], root))
                group = []
                for from_ref, to_ref in mine:
                    copy = pltpu.make_async_copy(from_ref, to_ref, done.at[used])
                    copy.start()
                    group.append(copy)
                    used += 1
                started.append(group)
        matrix = 0
        for i, (sources, _, left_stats, right_stats, _, weights, _) in enumerate(groups):
            rows, columns = left_stats.shape[2], right_stats.shape[2]
            high, wide = left_stats.shape[1], right_stats.shape[1]
            shard_ref, left_ref, right_ref, root_ref = smalls[:4]
            weight_ref = None if weights is None else smalls[4]
            smalls = smalls[4 if weights is None else 5 :]
            left_out, right_out, third_out = outs[3 * i : 3 * i + 3]
            lane = lax.broadcasted_iota(jnp.int32, (wide, columns), 1)
            row = lax.broadcasted_iota(jnp.int32, (wide, columns), 0)
            pick = (lane == row + index * wide).astype(F32)
            for j in range(len(sources)):
                for copy in started[matrix]:
                    copy.wait()
                whole = scratches[2 * matrix][...].reshape(rows, columns)
                other = scratches[2 * matrix + 1][...]
                matrix += 1
                stacked = [shard_ref[j], pick] + ([root_ref[j]] if weights is None else [])
                first = against(jnp.concatenate(stacked, axis=0).astype(BF16), whole)
                left_out[j] = 0.5 * left_ref[j] + (0.5 / columns) * first[:high]
                picked = first[high : high + wide]
                if weights is None:
                    second = product(picked.astype(BF16), whole)
                    right_out[j] = 0.5 * right_ref[j] + (0.5 / rows) * second
                    turned = first[high + wide :].astype(BF16)
                    third_out[j] = product(turned, other).astype(BF16)
                else:
                    stacked = jnp.concatenate([root_ref[j], picked], axis=0).astype(BF16)
                    second = product(stacked, whole)
                    right_out[j] = 0.5 * right_ref[j] + (0.5 / rows) * second[high:]
                    step = product(second[:high].astype(BF16), other)
                    third_out[j] = weight_ref[j] - step * (1.0 / math.sqrt(rows))

    vmem = pl.BlockSpec(memory_space=pltpu.VMEM)
    results = pl.pallas_call(
        kernel,
        out_shape=out_shape,
        in_specs=[pl.BlockSpec(memory_space=pltpu.SMEM)]
        + [pl.BlockSpec(memory_space=pl.ANY)] * len(big)
        + [vmem] * len(small),
        out_specs=[vmem] * len(out_shape),
        scratch_shapes=scratch + [pltpu.SemaphoreType.DMA((copies,))],
        compiler_params=pltpu.CompilerParams(vmem_limit_bytes=56 << 20),
    )(bits, *big, *small)
    return [results[3 * i : 3 * i + 3] for i in range(len(groups))]


def body(
    embedding,
    latent,
    segment_ids,
    cotangent,
    weight_adapt,
    weight_attn,
    weight_gateup,
    weight_down,
    norm_gains,
    left_adapt,
    right_adapt,
    left_attn,
    right_attn,
    left_gateup,
    right_gateup,
    left_down,
    right_down,
    left_root_adapt,
    right_root_adapt,
    left_root_attn,
    right_root_attn,
    left_root_gateup,
    right_root_gateup,
    left_root_down,
    right_root_down,
    gain_moment,
):
    n_dp, n_seq = lax.axis_size("dp"), lax.axis_size("seq")
    links = Links(n_dp, n_seq)
    seq_count, group_len, width = embedding.shape
    tokens = seq_count * group_len
    length = group_len * n_seq
    hidden_width = weight_gateup.shape[2]
    by_heads = HEADS % n_seq == 0

    gain_share = norm_gains.shape[1]
    small = jnp.concatenate(
        [norm_gains.astype(BF16).reshape(-1), segment_ids.astype(BF16).reshape(-1)]
    )
    small = jnp.pad(small[None], ((0, 7), (0, width - small.shape[0])))
    attn_rows = weight_attn.astype(BF16)
    first = Gathering(links, [weight_adapt.astype(BF16), small])
    second = Gathering(links, [attn_rows[i] for i in range(4)])
    third = Gathering(links, [weight_down.astype(BF16)])
    gateup_rows = weight_gateup.astype(BF16)
    gateup_rows = jnp.concatenate([gateup_rows[0], gateup_rows[1]], axis=1)
    inner_steps, cross_steps = range(len(links.inner)), range(links.steps)
    for step in inner_steps:
        first.inside(step)
    (gateup_rows,) = tick([first, second], gateup_rows)
    gateup_full = lax.all_gather(gateup_rows, AXES, axis=0, tiled=True)
    for step in inner_steps:
        second.inside(step)
    for step in cross_steps:
        first.cross(step)
    tick([first, second, third])
    first.core()
    adapt_full, small = first.finish()
    for step in cross_steps:
        second.cross(step)
    for step in inner_steps:
        third.inside(step)
    tick([second, third])
    second.core()
    query_full, key_full, value_full, out_full = second.finish()
    for step in cross_steps:
        third.cross(step)
    third.core()
    (down_full,) = third.finish()

    small = small.reshape(links.count, 8, width)[:, 0]
    gain_values = small[:, : 4 * gain_share].reshape(links.count, 4, gain_share)
    gain_values = gain_values.transpose(1, 0, 2).reshape(4, width).astype(F32)
    ids = small[:, 4 * gain_share : 4 * gain_share + tokens].reshape(n_dp, n_seq, seq_count, -1)
    ids = lax.dynamic_index_in_dim(ids, lax.axis_index("dp"), 0, False)
    segment_whole = ids.transpose(1, 0, 2).reshape(seq_count, length).astype(jnp.int32)

    all_places = jnp.arange(length, dtype=jnp.int32)
    doc_starts = jnp.sum(
        (segment_whole[:, None, :] < segment_whole[:, :, None]).astype(jnp.int32), axis=2
    )
    places = all_places[None, :] - doc_starts
    half_dim = HEAD_DIM // 2
    frequency = THETA ** (-jnp.arange(half_dim, dtype=F32) / half_dim)
    angles = places.astype(F32)[..., None] * frequency
    cosine_all, sine_all = jnp.cos(angles), jnp.sin(angles)
    own_start = links.seq_index * group_len
    cosine = lax.dynamic_slice_in_dim(cosine_all, own_start, group_len, 1)
    sine_table = lax.dynamic_slice_in_dim(sine_all, own_start, group_len, 1)
    if by_heads:
        query_places, segment_query = all_places, segment_whole
        cosine_back, sine_back = cosine_all[:, None], sine_all[:, None]
    else:
        query_places, segment_query = own_start + jnp.arange(group_len), segment_ids
        cosine_back, sine_back = cosine[:, None], sine_table[:, None]
    allowed = (all_places[None, None, :] <= query_places[None, :, None]) & (
        segment_whole[:, None, :] == segment_query[:, :, None]
    )

    def to_heads(values):
        parts = values.shape[2]
        values = values.transpose(3, 2, 0, 1, 4)
        came = lax.all_to_all(values, "seq", 0, 0, tiled=True)
        came = came.reshape(n_seq, HEADS // n_seq, parts, seq_count, group_len, HEAD_DIM)
        came = came.transpose(2, 3, 1, 0, 4, 5)
        return came.reshape(parts, seq_count, HEADS // n_seq, length, HEAD_DIM)

    def to_tokens(values):
        parts = values.shape[0]
        own = HEADS // n_seq
        values = values.reshape(parts, seq_count, own, n_seq, group_len, HEAD_DIM)
        values = values.transpose(3, 2, 0, 1, 4, 5)
        came = lax.all_to_all(values, "seq", 0, 0, tiled=True)
        came = came.reshape(HEADS, parts, seq_count, group_len, HEAD_DIM)
        return came.transpose(1, 2, 3, 0, 4)

    scaling = 1.0 / math.sqrt(HEAD_DIM)

    def attention(queries, keys, values):
        if by_heads:
            queries, keys, values = to_heads(jnp.stack([queries, keys, values], axis=2))
        else:
            queries = queries.transpose(0, 2, 1, 3)
            keys, values = (
                lax.all_gather(item, "seq", axis=1, tiled=True).transpose(0, 2, 1, 3)
                for item in (keys, values)
            )
        scores = jnp.einsum("shqd,shkd->shqk", queries, keys, preferred_element_type=F32)
        scores = jnp.where(allowed[:, None], scores * scaling, -1e30)
        exponent = jnp.exp(scores - jnp.max(scores, axis=-1, keepdims=True))
        soft_full = exponent / jnp.sum(exponent, axis=-1, keepdims=True)
        mixed = jnp.einsum(
            "shqk,shkd->shqd", soft_full.astype(BF16), values, preferred_element_type=F32
        ).astype(BF16)
        if by_heads:
            mixed = to_tokens(mixed[None])[0]
        else:
            mixed = mixed.transpose(0, 2, 1, 3)
        return mixed.reshape(tokens, width), (queries, keys, values, soft_full)

    def attention_back(mixed_grad, saved):
        queries, keys, values, soft_full = saved
        soft_grad = jnp.einsum("shqd,shkd->shqk", mixed_grad, values, preferred_element_type=F32)
        inner_sum = jnp.sum(soft_full * soft_grad, axis=-1, keepdims=True)
        score_grad = (soft_full * (soft_grad - inner_sum)).astype(BF16)
        query_grad = (
            jnp.einsum("shqk,shkd->shqd", score_grad, keys, preferred_element_type=F32) * scaling
        )
        key_grad = (
            jnp.einsum("shqk,shqd->shkd", score_grad, queries, preferred_element_type=F32)
            * scaling
        )
        value_grad = jnp.einsum(
            "shqk,shqd->shkd", soft_full.astype(BF16), mixed_grad, preferred_element_type=F32
        )
        if by_heads:
            query_grad = rotate(query_grad, cosine_back, -sine_back).astype(BF16)
            key_grad = rotate(key_grad, cosine_back, -sine_back).astype(BF16)
            value_grad = value_grad.astype(BF16)
            return jnp.stack([query_grad, key_grad, value_grad])
        key_grad, value_grad = (
            lax.psum_scatter(item.astype(BF16), "seq", scatter_dimension=2, tiled=True).astype(F32)
            for item in (key_grad, value_grad)
        )
        query_grad = rotate(query_grad, cosine_back, -sine_back).astype(BF16)
        key_grad = rotate(key_grad, cosine_back, -sine_back).astype(BF16)
        grads = jnp.stack([query_grad, key_grad, value_grad.astype(BF16)])
        return grads.transpose(0, 1, 3, 2, 4)

    embed_flat = embedding.reshape(tokens, width)
    embed_part = product(embed_flat, adapt_full[width:])
    root_stack = jnp.concatenate(
        [
            right_root_adapt.astype(BF16)[:, None],
            right_root_attn.astype(BF16).transpose(1, 0, 2),
            right_root_down.astype(BF16)[:, None],
            left_root_gateup.astype(BF16).transpose(1, 0, 2),
        ],
        axis=1,
    )
    root_stack = root_stack.reshape(root_stack.shape[0], 8 * width)
    roots = []

    def forward(latent_low):
        start_sum = product(latent_low, adapt_full[:width]) + embed_part
        scale_one = norm_scale(start_sum)
        normed_one = (start_sum * scale_one * gain_values[0]).astype(BF16)
        head_shape = (seq_count, group_len, HEADS, HEAD_DIM)
        turn_cos, turn_sin = cosine[:, :, None, :], sine_table[:, :, None, :]
        queries = product(normed_one, query_full).reshape(head_shape)
        queries = rotate(queries, turn_cos, turn_sin).astype(BF16)
        keys = product(normed_one, key_full).reshape(head_shape)
        keys = rotate(keys, turn_cos, turn_sin).astype(BF16)
        values = product(normed_one, value_full).astype(BF16).reshape(head_shape)
        tied = len(roots) > 0
        if not tied:
            tied_stack, queries = tie(root_stack, queries)
            roots.append(lax.all_gather(tied_stack, AXES, axis=0, tiled=True))
        mixed_heads, attended = attention(queries, keys, values)
        if tied:
            roots[0], mixed_heads = tie(roots[0], mixed_heads)
        branch = product(mixed_heads, out_full)
        scale_two = norm_scale(branch)
        middle = start_sum + branch * scale_two * gain_values[1]
        scale_three = norm_scale(middle)
        normed_three = (middle * scale_three * gain_values[2]).astype(BF16)
        both = product(normed_three, gateup_full)
        gate_value, upward = both[:, :hidden_width], both[:, hidden_width:]
        hidden = (jax.nn.silu(gate_value) * upward).astype(BF16)
        feed_out = product(hidden, down_full)
        scale_four = norm_scale(feed_out)
        result = middle + feed_out * scale_four * gain_values[3]
        saved_values = (
            start_sum,
            scale_one,
            normed_one,
            attended,
            mixed_heads,
            branch,
            scale_two,
            middle,
            scale_three,
            normed_three,
            gate_value,
            upward,
            hidden,
            feed_out,
            scale_four,
        )
        return (result, saved_values)

    latent_low = latent.reshape(tokens, width)
    latent_state, unused_saved = forward(latent_low)
    latent_low = latent_state.astype(BF16)
    final_state, saved_values = forward(latent_low)
    (
        start_sum,
        scale_one,
        normed_one,
        attended,
        mixed_heads,
        branch,
        scale_two,
        middle,
        scale_three,
        normed_three,
        gate_value,
        upward,
        hidden,
        feed_out,
        scale_four,
    ) = saved_values
    factor = 1.0 / math.sqrt(seq_count * n_dp * length)
    incoming = cotangent.astype(F32).reshape(tokens, width)
    feed_grad, gain_four = norm_back(feed_out, scale_four, gain_values[3], incoming)
    feed_grad = feed_grad.astype(BF16)
    down_sum = Reduction(links, width)
    hidden_pair = down_sum.early(hidden)
    normed_three_pair = down_sum.early(normed_three)
    mixed_pair = down_sum.early(mixed_heads)
    normed_one_pair = down_sum.early(normed_one)
    joined_pair = down_sum.early(jnp.concatenate([latent_low, embed_flat], axis=1))
    down_sum.send(hidden_pair, feed_grad)
    hidden_grad = against(feed_grad, down_full)
    gate_grad = (hidden_grad * upward * silu_grad(gate_value)).astype(BF16)
    up_grad = (hidden_grad * jax.nn.silu(gate_value)).astype(BF16)
    gateup_sum = Reduction(links, hidden_width)
    gateup_sum.send(normed_three_pair, gate_grad)
    gateup_sum.send(normed_three_pair, up_grad)
    both_grad = jnp.concatenate([gate_grad, up_grad], axis=1)
    normed_three_grad = against(both_grad, gateup_full)
    middle_grad, gain_three = norm_back(middle, scale_three, gain_values[2], normed_three_grad)
    middle_grad = middle_grad + incoming
    branch_grad, gain_two = norm_back(branch, scale_two, gain_values[1], middle_grad)
    branch_grad = branch_grad.astype(BF16)
    mixed_grad = against(branch_grad, out_full).astype(BF16)
    rest_sum = Reduction(links, width)
    rest_sum.send(mixed_pair, branch_grad)
    down_sum.add()
    (mixed_grad,) = tick([down_sum], mixed_grad)
    mixed_grad = mixed_grad.reshape(seq_count, group_len, HEADS, HEAD_DIM)
    if by_heads:
        mixed_grad = to_heads(mixed_grad[:, :, None])[0]
    else:
        mixed_grad = mixed_grad.transpose(0, 2, 1, 3)
    down_sum.cross(0)
    gateup_sum.add()
    gateup_sum.cross(0)
    (mixed_grad,) = tick([down_sum], mixed_grad)
    grads = attention_back(mixed_grad, attended)
    for step in cross_steps[1:]:
        down_sum.cross(step)
        gateup_sum.cross(step)
    if by_heads:
        grads = to_tokens(grads)
    query_pre, key_pre, value_pre = grads.reshape(3, tokens, width)
    query_pre, key_pre, value_pre = tick([down_sum], query_pre, key_pre, value_pre)
    rest_sum.send(normed_one_pair, jnp.concatenate([query_pre, key_pre, value_pre], axis=1))
    normed_one_grad = (
        against(query_pre, query_full) + against(key_pre, key_full) + against(value_pre, value_full)
    )
    start_grad, gain_one = norm_back(start_sum, scale_one, gain_values[0], normed_one_grad)
    start_grad = (start_grad + middle_grad).astype(BF16)
    rest_sum.send(joined_pair, start_grad)
    gain_sums = jnp.stack([gain_one, gain_two, gain_three, gain_four])
    gain_sums = gain_sums.reshape(4, links.count, gain_share).transpose(1, 0, 2)
    gain_sums = gain_sums.reshape(links.count, 1, 4 * gain_share)
    gain_sums = jnp.pad(gain_sums, ((0, 0), (0, 7), (0, width - 4 * gain_share)))
    rest_sum.send_rows(gain_sums.reshape(-1, width))
    rest_sum.add()
    root_rows = roots[0]
    (start_grad,) = tick([down_sum, rest_sum], start_grad)
    rest_sum.cross(0)
    for step in inner_steps:
        gateup_sum.inside(step)
    tick([rest_sum, gateup_sum])
    gate_shards = (gateup_sum.parts[0] * factor).reshape(2, -1, hidden_width)
    full_both = lax.all_gather(
        jnp.concatenate([gate_shards[0], gate_shards[1]], axis=1).astype(BF16),
        AXES,
        axis=0,
        tiled=True,
    )
    for step in cross_steps[1:]:
        rest_sum.cross(step)
    for step in inner_steps:
        down_sum.inside(step)
    tick([rest_sum, down_sum])
    reduced_down = down_sum.parts[0] * factor
    first = Gathering(links, [reduced_down.astype(BF16)])
    left_root_adapt, left_root_attn, left_root_down, right_root_gateup, reduced_down = tie(
        left_root_adapt, left_root_attn, left_root_down, right_root_gateup, reduced_down
    )
    rest_sum.inside(0)
    first.inside(0)
    tick([rest_sum, first])
    for step in inner_steps[1:]:
        rest_sum.inside(step)
        first.inside(step)
    tick([rest_sum, first])
    reduced_rest = rest_sum.parts[0] * factor
    row_share = width // links.count
    attn_shards = reduced_rest[: 4 * row_share].reshape(4, row_share, width)
    attn_shards = jnp.concatenate([attn_shards[1:], attn_shards[:1]], axis=0)
    reduced_adapt = reduced_rest[4 * row_share : 6 * row_share]
    reduced_gains = reduced_rest[6 * row_share, : 4 * gain_share].reshape(4, gain_share)
    third = Gathering(
        links, [attn_shards[i].astype(BF16) for i in range(4)] + [reduced_adapt.astype(BF16)]
    )
    third.inside(0)
    first.cross(0)
    (full_both,) = tick([third, first], full_both)
    def statistics(shard, whole, left_stat, right_stat, left_root):
        rows, columns = whole.shape
        new_left = 0.5 * left_stat + (0.5 / columns) * against(shard.astype(BF16), whole)
        count = right_stat.shape[0]
        own = lax.dynamic_slice_in_dim(whole, links.index * count, count, 1).T
        if left_root is None:
            return (new_left, 0.5 * right_stat + (0.5 / rows) * product(own, whole), None)
        own_count = left_root.shape[0]
        both = product(jnp.concatenate([left_root.astype(BF16), own], axis=0), whole)
        return (new_left, 0.5 * right_stat + (0.5 / rows) * both[own_count:], both[:own_count])

    def whole_step(part, which, rows):
        root = root_rows[:, which * width : (which + 1) * width]
        return product(part.astype(BF16), root) * (1.0 / math.sqrt(rows))

    for step in inner_steps[1:]:
        third.inside(step)
    for step in cross_steps[1:]:
        first.cross(step)
    fits = row_share % 16 == 0
    if fits:
        sources = [Source([full_both], i * hidden_width, width, hidden_width) for i in range(2)]
        ((new_left_gateup, new_right_gateup, step_columns),) = shampoo(
            links,
            [
                (
                    sources,
                    gate_shards,
                    left_gateup,
                    right_gateup,
                    right_root_gateup,
                    None,
                    [6, 7],
                )
            ],
            root_rows,
        )
        step_columns = step_columns.transpose(0, 2, 1)
    else:
        whole_gates = [full_both[:, :hidden_width], full_both[:, hidden_width:]]
        gateup_parts = [
            statistics(gate_shards[i], whole_gates[i], left_gateup[i], right_gateup[i], None)
            for i in range(2)
        ]
        step_columns = []
        for i in range(2):
            turned = against(whole_gates[i], right_root_gateup[i].astype(BF16)).astype(BF16)
            root = root_rows[:, (6 + i) * width : (7 + i) * width]
            step_columns.append(product(root, turned).astype(BF16))
        step_columns = jnp.stack(step_columns)
        new_left_gateup = jnp.stack([member[0] for member in gateup_parts])
        new_right_gateup = jnp.stack([member[1] for member in gateup_parts])
    ff_share = step_columns.shape[2]
    step_columns = step_columns.reshape(2, links.count, row_share, ff_share).transpose(1, 0, 2, 3)
    (step_columns,) = tick([third, first], step_columns)
    first.core()
    step_rows = lax.all_to_all(step_columns, AXES, 0, 0, tiled=True)
    step_gateup = step_rows.transpose(1, 2, 0, 3).reshape(2, row_share, hidden_width)
    new_gateup = weight_gateup - step_gateup.astype(F32) * (1.0 / math.sqrt(width))

    third.cross(0)
    (new_gateup,) = tick([third, first], new_gateup)
    for step in cross_steps[1:]:
        third.cross(step)
    if fits:
        down_group = (
            first.sources(),
            reduced_down[None],
            left_down[None],
            right_down[None],
            left_root_down[None],
            weight_down[None],
            [5],
        )
        ((new_left_down, new_right_down, new_down),) = shampoo(links, [down_group], root_rows)
        new_left_down, new_right_down, new_down = new_left_down[0], new_right_down[0], new_down[0]
    else:
        (full_down,) = first.finish()
        new_left_down, new_right_down, down_part = statistics(
            reduced_down, full_down, left_down, right_down, left_root_down
        )
        new_down = weight_down - whole_step(down_part, 5, hidden_width)
    (new_down,) = tick([third], new_down)
    third.core()
    tick([third])
    grad_embedding = against(start_grad, adapt_full[width:]).reshape(
        seq_count, group_len, width
    )
    if fits:
        sources = third.sources()
        attn_group = (
            sources[:4],
            attn_shards,
            left_attn,
            right_attn,
            left_root_attn,
            weight_attn,
            [1, 2, 3, 4],
        )
        adapt_group = (
            sources[4:],
            reduced_adapt[None],
            left_adapt[None],
            right_adapt[None],
            left_root_adapt[None],
            weight_adapt[None],
            [0],
        )
        (
            (new_left_attn, new_right_attn, new_attn),
            (new_left_adapt, new_right_adapt, new_adapt),
        ) = shampoo(links, [attn_group, adapt_group], root_rows)
        new_left_adapt, new_right_adapt, new_adapt = (
            new_left_adapt[0],
            new_right_adapt[0],
            new_adapt[0],
        )
    else:
        *attn_wholes, full_adapt = third.finish()
        attn_parts = [
            statistics(
                attn_shards[i], attn_wholes[i], left_attn[i], right_attn[i], left_root_attn[i]
            )
            for i in range(4)
        ]
        new_attn = weight_attn - jnp.stack(
            [whole_step(attn_parts[i][2], 1 + i, width) for i in range(4)]
        )
        new_left_attn = jnp.stack([member[0] for member in attn_parts])
        new_right_attn = jnp.stack([member[1] for member in attn_parts])
        new_left_adapt, new_right_adapt, adapt_part = statistics(
            reduced_adapt, full_adapt, left_adapt, right_adapt, left_root_adapt
        )
        new_adapt = weight_adapt - whole_step(adapt_part, 0, 2 * width)
    new_gain_moment = 0.5 * gain_moment + 0.5 * reduced_gains * reduced_gains
    new_norm_gains = norm_gains - 0.5 * reduced_gains / (jnp.sqrt(new_gain_moment) + 1e-08)
    latent_out = final_state.reshape(seq_count, group_len, width).astype(BF16)
    return (
        latent_out,
        grad_embedding,
        reduced_adapt,
        attn_shards,
        gate_shards,
        reduced_down,
        reduced_gains,
        new_left_adapt,
        new_right_adapt,
        new_left_attn,
        new_right_attn,
        new_left_gateup,
        new_right_gateup,
        new_left_down,
        new_right_down,
        new_adapt,
        new_attn,
        new_gateup,
        new_down,
        new_gain_moment,
        new_norm_gains,
    )

def solution(mesh):
    return jax.shard_map(
        body,
        mesh=mesh,
        in_specs=(
            P("dp", "seq", None),
            P("dp", "seq", None),
            P("dp", "seq"),
            P("dp", "seq", None),
            P(("dp", "seq"), None),
            P(None, ("dp", "seq"), None),
            P(None, ("dp", "seq"), None),
            P(("dp", "seq"), None),
            P(None, ("dp", "seq")),
            P(("dp", "seq"), None),
            P(("dp", "seq"), None),
            P(None, ("dp", "seq"), None),
            P(None, ("dp", "seq"), None),
            P(None, ("dp", "seq"), None),
            P(None, ("dp", "seq"), None),
            P(("dp", "seq"), None),
            P(("dp", "seq"), None),
            P(("dp", "seq"), None),
            P(("dp", "seq"), None),
            P(None, ("dp", "seq"), None),
            P(None, ("dp", "seq"), None),
            P(None, ("dp", "seq"), None),
            P(None, ("dp", "seq"), None),
            P(("dp", "seq"), None),
            P(("dp", "seq"), None),
            P(None, ("dp", "seq")),
        ),
        out_specs=(
            P("dp", "seq", None),
            P("dp", "seq", None),
            P(("dp", "seq"), None),
            P(None, ("dp", "seq"), None),
            P(None, ("dp", "seq"), None),
            P(("dp", "seq"), None),
            P(None, ("dp", "seq")),
            P(("dp", "seq"), None),
            P(("dp", "seq"), None),
            P(None, ("dp", "seq"), None),
            P(None, ("dp", "seq"), None),
            P(None, ("dp", "seq"), None),
            P(None, ("dp", "seq"), None),
            P(("dp", "seq"), None),
            P(("dp", "seq"), None),
            P(("dp", "seq"), None),
            P(None, ("dp", "seq"), None),
            P(None, ("dp", "seq"), None),
            P(("dp", "seq"), None),
            P(None, ("dp", "seq")),
            P(None, ("dp", "seq")),
        ),
        check_vma=False,
    )
```

```python
import math

import jax
import jax.numpy as jnp
from jax import lax
from jax.experimental import pallas as pl
from jax.experimental.pallas import tpu as pltpu
from jax.sharding import PartitionSpec as P

HEADS = 8
HEAD_DIM = 128
EPSILON = 1e-06
THETA = 50000.0
AXES = ("dp", "seq")
BF16 = jnp.bfloat16
F32 = jnp.float32


def product(left_side, right_side):
    return jnp.dot(left_side, right_side, preferred_element_type=F32)


def across(left_side, right_side):
    return lax.dot_general(
        left_side, right_side, (((0,), (0,)), ((), ())), preferred_element_type=F32
    )


def against(left_side, right_side):
    return lax.dot_general(
        left_side, right_side, (((1,), (1,)), ((), ())), preferred_element_type=F32
    )


def norm_scale(values):
    return lax.rsqrt(jnp.mean(values * values, axis=-1, keepdims=True) + EPSILON)


def norm_back(values, scaling, gain_row, gradient):
    unit_rows = values * scaling
    weighted = gradient * gain_row
    moved = scaling * (
        weighted - unit_rows * jnp.mean(unit_rows * weighted, axis=-1, keepdims=True)
    )
    return (moved, jnp.sum(gradient * unit_rows, axis=0))


def rotate(values, cosine, sine_table):
    half_dim = values.shape[-1] // 2
    first_half = values[..., :half_dim]
    second_half = values[..., half_dim:]
    return jnp.concatenate(
        [
            first_half * cosine - second_half * sine_table,
            second_half * cosine + first_half * sine_table,
        ],
        axis=-1,
    )


def silu_grad(values):
    sigmoid_value = jax.nn.sigmoid(values)
    return sigmoid_value * (1.0 + values * (1.0 - sigmoid_value))


def tie(*values):
    return lax.optimization_barrier(values)


def tick(works, *values):
    flat = [part for work in works for part in work.parts]
    tied = list(lax.optimization_barrier(tuple(flat) + values))
    for work in works:
        count = len(work.parts)
        work.parts, tied = tied[:count], tied[count:]
    return tied


class Links:
    def __init__(self, n_dp, n_seq):
        self.count = n_dp * n_seq
        self.bits = (self.count - 1).bit_length()
        self.core = (n_dp - 1).bit_length() - 1
        self.last = self.bits - 1
        self.upper = list(range(self.core))
        self.inner = list(range(self.core + 1, self.last))
        self.index = lax.axis_index("dp") * n_seq + lax.axis_index("seq")
        self.seq_index = lax.axis_index("seq")
        self.pairs = [
            [(i, i ^ (1 << (self.bits - 1 - bit))) for i in range(self.count)]
            for bit in range(self.bits)
        ]
        self.steps = len(self.upper) + 1

    def own(self, bit):
        return (self.index >> (self.bits - 1 - bit)) & 1

    def swap(self, values, bit):
        return lax.ppermute(values, AXES, self.pairs[bit])


class Gathering:
    def __init__(self, links, shards):
        self.links = links
        self.heights = [shard.shape[0] for shard in shards]
        self.rows = sum(self.heights)
        shard = shards[0] if len(shards) == 1 else jnp.concatenate(shards, axis=0)
        self.parts = [shard]
        self.known = [[]]

    def widen(self, i, bit):
        links, part, known = self.links, self.parts[i], self.known[i]
        came = links.swap(part, bit)
        columns = part.shape[1]
        before = 1 << sum(1 for other in known if other < bit)
        mine = part.reshape(before, 1, -1, columns)
        both = jnp.zeros((before, 2) + mine.shape[2:], part.dtype)
        both = lax.dynamic_update_slice(both, mine, (0, links.own(bit), 0, 0))
        both = lax.dynamic_update_slice(
            both, came.reshape(mine.shape), (0, 1 - links.own(bit), 0, 0)
        )
        self.parts[i] = both.reshape(-1, columns)
        self.known[i] = known + [bit]

    def inside(self, step):
        self.widen(0, self.links.inner[step])

    def cross(self, step):
        links = self.links
        if len(self.parts) == 1:
            half = self.parts[0].shape[1] // 2
            self.parts = [self.parts[0][:, :half], self.parts[0][:, half:]]
            self.known = [self.known[0], self.known[0]]
        orders = ([links.last] + links.upper, links.upper + [links.last])
        for i in range(2):
            self.widen(i, orders[i][step])

    def core(self):
        self.parts += [self.links.swap(part, self.links.core) for part in self.parts]

    def finish(self):
        links = self.links
        before, half = 1 << len(links.upper), self.parts[0].shape[1]
        four = [part.reshape(before, -1, self.rows, half) for part in self.parts]
        wholes, row = [], 0
        for height in self.heights:
            piece = [part[:, :, row : row + height] for part in four]
            own = links.own(links.core)
            whole = jnp.zeros((before, 2) + piece[0].shape[1:3] + (2 * half,), piece[0].dtype)
            for i in range(4):
                place = own if i < 2 else 1 - own
                whole = lax.dynamic_update_slice(
                    whole, piece[i][:, None], (0, place, 0, 0, (i % 2) * half)
                )
            wholes.append(whole.reshape(-1, 2 * half))
            row += height
        return wholes

    def sources(self):
        columns = 2 * self.parts[0].shape[1]
        befores = 1 << len(self.links.upper)
        if len(self.heights) == 1:
            arrays = [part.reshape(befores, -1, part.shape[1]) for part in self.parts]
            return [Source(arrays, 0, arrays[0].shape[1], columns)]
        arrays = [part.reshape(-1, self.rows, part.shape[1]) for part in self.parts]
        sources, row = [], 0
        for height in self.heights:
            sources.append(Source(arrays, row, height, columns))
            row += height
        return sources


class Reduction:
    def __init__(self, links, wide):
        self.links, self.wide = links, wide
        self.terms = []

    def sides(self, left_side, which):
        blocks = 2 << len(self.links.upper)
        wide = left_side.shape[1] // blocks
        chosen = []
        for block in range(0, blocks, 2):
            first = left_side[:, block * wide : (block + 1) * wide]
            second = left_side[:, (block + 1) * wide : (block + 2) * wide]
            chosen.append(jnp.where(which == 0, first, second))
        return jnp.concatenate(chosen, axis=1)

    def early(self, left_side):
        links = self.links
        away = self.sides(left_side, 1 - links.own(links.core))
        kept = self.sides(left_side, links.own(links.core))
        return (kept, links.swap(away, links.core))

    def send(self, left_pair, right_side):
        other = self.links.swap(right_side, self.links.core)
        left_both = jnp.concatenate(left_pair, axis=0)
        self.terms.append(lambda: across(left_both, jnp.concatenate([right_side, other], axis=0)))

    def send_rows(self, values):
        links = self.links
        halves = values.reshape(1 << len(links.upper), 2, -1, values.shape[1])
        own = links.own(links.core)
        away = lax.dynamic_index_in_dim(halves, 1 - own, 1, False).reshape(-1, values.shape[1])
        kept = lax.dynamic_index_in_dim(halves, own, 1, False).reshape(-1, values.shape[1])
        came = links.swap(away.astype(BF16), links.core)
        self.terms.append(lambda: kept + came.astype(F32))

    def add(self):
        links = self.links
        owners = links.count // 2
        total = []
        for term in self.terms:
            item = term().astype(BF16)
            item = item.reshape(owners, -1, item.shape[1])
            for start in range(0, item.shape[2], self.wide):
                total.append(item[:, :, start : start + self.wide])
        total = total[0] if len(total) == 1 else jnp.concatenate(total, axis=1)
        total = total.reshape(-1, total.shape[2])
        half = total.shape[1] // 2
        self.parts = [total[:, :half], total[:, half:]]
        left = [bit for bit in range(links.bits) if bit != links.core]
        self.left = [list(left), list(left)]

    def halve(self, i, bit, out_type=BF16):
        links, part = self.links, self.parts[i]
        columns = part.shape[1]
        before = 1 << sum(1 for other in self.left[i] if other < bit)
        both = part.reshape(before, 2, -1, columns)
        own = links.own(bit)
        away = lax.dynamic_index_in_dim(both, 1 - own, 1, False)
        kept = lax.dynamic_index_in_dim(both, own, 1, False)
        came = links.swap(away.reshape(-1, columns), bit)
        kept = kept.reshape(-1, columns).astype(F32) + came.astype(F32)
        self.parts[i] = kept.astype(out_type)
        self.left[i].remove(bit)

    def cross(self, step):
        links = self.links
        orders = (links.upper + [links.last], [links.last] + links.upper)
        for i in range(2):
            self.halve(i, orders[i][step])

    def join(self, other):
        owners = 1 << len(self.left[0])
        for i in range(2):
            both = [part.reshape(owners, -1, part.shape[1]) for part in (self.parts[i], other.parts[i])]
            self.parts[i] = jnp.concatenate(both, axis=1).reshape(-1, both[0].shape[2])

    def inside(self, step):
        if len(self.parts) == 2:
            self.parts = [jnp.concatenate(self.parts, axis=1)]
        final = step == len(self.links.inner) - 1
        self.halve(0, self.links.inner[-1 - step], F32 if final else BF16)


class Source:
    def __init__(self, arrays, start, height, columns):
        self.arrays, self.start, self.height, self.columns = arrays, start, height, columns


def shampoo(links, groups, roots):
    side = roots.shape[0]
    befores = 1 << len(links.upper)
    big = [roots]
    for sources, *_ in groups:
        for source in sources:
            for array in source.arrays:
                if not any(array is other for other in big):
                    big.append(array)
    place = {id(array): i for i, array in enumerate(big)}
    small, out_shape, scratch, copies = [], [], [], 0
    for sources, shards, left_stats, right_stats, own_roots, weights, which in groups:
        count, _, rows = left_stats.shape
        columns = right_stats.shape[2]
        small += [shards, left_stats, right_stats, own_roots]
        small += [] if weights is None else [weights]
        third = (count, right_stats.shape[1], rows) if weights is None else weights.shape
        out_shape += [
            jax.ShapeDtypeStruct(left_stats.shape, F32),
            jax.ShapeDtypeStruct(right_stats.shape, F32),
            jax.ShapeDtypeStruct(third, BF16 if weights is None else F32),
        ]
        for source in sources:
            if len(source.arrays) == 1:
                scratch.append(pltpu.VMEM((1, rows, columns), BF16))
                copies += 2
            else:
                blocks = 2 * source.arrays[0].shape[0]
                scratch.append(pltpu.VMEM((blocks, rows // blocks, columns), BF16))
                copies += 4 * befores + 1
            scratch.append(pltpu.VMEM((side, side), BF16))
    bits = jnp.stack([links.index, links.own(links.core)]).astype(jnp.int32)

    def kernel(*refs):
        place_ref, refs = refs[0], list(refs[1:])
        bigs, refs = refs[: len(big)], refs[len(big) :]
        smalls, refs = refs[: len(small)], refs[len(small) :]
        outs, refs = refs[: len(out_shape)], refs[len(out_shape) :]
        scratches, done = refs[: len(scratch)], refs[-1]
        index, own = place_ref[0], place_ref[1]
        started, used = [], 0
        for sources, *_, which in groups:
            for source, block in zip(sources, which):
                whole, root = scratches[2 * len(started)], scratches[2 * len(started) + 1]
                mine = []
                if len(source.arrays) == 1:
                    ref = bigs[place[id(source.arrays[0])]]
                    mine.append((ref.at[:, pl.ds(source.start, source.columns)], whole.at[0]))
                else:
                    deep = source.arrays[0].shape[0] // befores
                    half = source.arrays[0].shape[2]
                    for part in range(4):
                        ref = bigs[place[id(source.arrays[part])]]
                        core = own if part < 2 else 1 - own
                        for before in range(befores):
                            from_ref = ref.at[
                                pl.ds(before * deep, deep), pl.ds(source.start, source.height)
                            ]
                            to_ref = whole.at[
                                pl.ds((2 * before + core) * deep, deep),
                                :,
                                pl.ds((part % 2) * half, half),
                            ]
                            mine.append((from_ref, to_ref))
                mine.append((bigs[0].at[:, pl.ds(block * side, side)], root))
                group = []
                for from_ref, to_ref in mine:
                    copy = pltpu.make_async_copy(from_ref, to_ref, done.at[used])
                    copy.start()
                    group.append(copy)
                    used += 1
                started.append(group)
        matrix = 0
        for i, (sources, _, left_stats, right_stats, _, weights, _) in enumerate(groups):
            rows, columns = left_stats.shape[2], right_stats.shape[2]
            high, wide = left_stats.shape[1], right_stats.shape[1]
            shard_ref, left_ref, right_ref, root_ref = smalls[:4]
            weight_ref = None if weights is None else smalls[4]
            smalls = smalls[4 if weights is None else 5 :]
            left_out, right_out, third_out = outs[3 * i : 3 * i + 3]
            lane = lax.broadcasted_iota(jnp.int32, (wide, columns), 1)
            row = lax.broadcasted_iota(jnp.int32, (wide, columns), 0)
            pick = (lane == row + index * wide).astype(F32)
            for j in range(len(sources)):
                for copy in started[matrix]:
                    copy.wait()
                whole = scratches[2 * matrix][...].reshape(rows, columns)
                other = scratches[2 * matrix + 1][...]
                matrix += 1
                stacked = [shard_ref[j], pick] + ([root_ref[j]] if weights is None else [])
                first = against(jnp.concatenate(stacked, axis=0).astype(BF16), whole)
                left_out[j] = 0.5 * left_ref[j] + (0.5 / columns) * first[:high]
                picked = first[high : high + wide]
                if weights is None:
                    second = product(picked.astype(BF16), whole)
                    right_out[j] = 0.5 * right_ref[j] + (0.5 / rows) * second
                    turned = first[high + wide :].astype(BF16)
                    third_out[j] = product(turned, other).astype(BF16)
                else:
                    stacked = jnp.concatenate([root_ref[j], picked], axis=0).astype(BF16)
                    second = product(stacked, whole)
                    right_out[j] = 0.5 * right_ref[j] + (0.5 / rows) * second[high:]
                    step = product(second[:high].astype(BF16), other)
                    third_out[j] = weight_ref[j] - step * (1.0 / math.sqrt(rows))

    vmem = pl.BlockSpec(memory_space=pltpu.VMEM)
    results = pl.pallas_call(
        kernel,
        out_shape=out_shape,
        in_specs=[pl.BlockSpec(memory_space=pltpu.SMEM)]
        + [pl.BlockSpec(memory_space=pl.ANY)] * len(big)
        + [vmem] * len(small),
        out_specs=[vmem] * len(out_shape),
        scratch_shapes=scratch + [pltpu.SemaphoreType.DMA((copies,))],
        compiler_params=pltpu.CompilerParams(vmem_limit_bytes=56 << 20),
    )(bits, *big, *small)
    return [results[3 * i : 3 * i + 3] for i in range(len(groups))]


def body(
    embedding,
    latent,
    segment_ids,
    cotangent,
    weight_adapt,
    weight_attn,
    weight_gateup,
    weight_down,
    norm_gains,
    left_adapt,
    right_adapt,
    left_attn,
    right_attn,
    left_gateup,
    right_gateup,
    left_down,
    right_down,
    left_root_adapt,
    right_root_adapt,
    left_root_attn,
    right_root_attn,
    left_root_gateup,
    right_root_gateup,
    left_root_down,
    right_root_down,
    gain_moment,
):
    n_dp, n_seq = lax.axis_size("dp"), lax.axis_size("seq")
    links = Links(n_dp, n_seq)
    seq_count, group_len, width = embedding.shape
    tokens = seq_count * group_len
    length = group_len * n_seq
    hidden_width = weight_gateup.shape[2]
    by_heads = HEADS % n_seq == 0

    gain_share = norm_gains.shape[1]
    small = jnp.concatenate(
        [norm_gains.astype(BF16).reshape(-1), segment_ids.astype(BF16).reshape(-1)]
    )
    small = jnp.pad(small[None], ((0, 7), (0, width - small.shape[0])))
    attn_rows = weight_attn.astype(BF16)
    first = Gathering(links, [weight_adapt.astype(BF16), small])
    second = Gathering(links, [attn_rows[i] for i in range(4)])
    third = Gathering(links, [weight_down.astype(BF16)])
    gateup_rows = weight_gateup.astype(BF16)
    gateup_rows = jnp.concatenate([gateup_rows[0], gateup_rows[1]], axis=1)
    inner_steps, cross_steps = range(len(links.inner)), range(links.steps)
    for step in inner_steps:
        first.inside(step)
    (gateup_rows,) = tick([first, second], gateup_rows)
    gateup_full = lax.all_gather(gateup_rows, AXES, axis=0, tiled=True)
    for step in inner_steps:
        second.inside(step)
    for step in cross_steps:
        first.cross(step)
    tick([first, second, third])
    first.core()
    adapt_full, small = first.finish()
    for step in cross_steps:
        second.cross(step)
    for step in inner_steps:
        third.inside(step)
    tick([second, third])
    second.core()
    query_full, key_full, value_full, out_full = second.finish()
    for step in cross_steps:
        third.cross(step)
    third.core()
    (down_full,) = third.finish()

    small = small.reshape(links.count, 8, width)[:, 0]
    gain_values = small[:, : 4 * gain_share].reshape(links.count, 4, gain_share)
    gain_values = gain_values.transpose(1, 0, 2).reshape(4, width).astype(F32)
    ids = small[:, 4 * gain_share : 4 * gain_share + tokens].reshape(n_dp, n_seq, seq_count, -1)
    ids = lax.dynamic_index_in_dim(ids, lax.axis_index("dp"), 0, False)
    segment_whole = ids.transpose(1, 0, 2).reshape(seq_count, length).astype(jnp.int32)

    all_places = jnp.arange(length, dtype=jnp.int32)
    doc_starts = jnp.sum(
        (segment_whole[:, None, :] < segment_whole[:, :, None]).astype(jnp.int32), axis=2
    )
    places = all_places[None, :] - doc_starts
    half_dim = HEAD_DIM // 2
    frequency = THETA ** (-jnp.arange(half_dim, dtype=F32) / half_dim)
    angles = places.astype(F32)[..., None] * frequency
    cosine_all, sine_all = jnp.cos(angles), jnp.sin(angles)
    own_start = links.seq_index * group_len
    cosine = lax.dynamic_slice_in_dim(cosine_all, own_start, group_len, 1)
    sine_table = lax.dynamic_slice_in_dim(sine_all, own_start, group_len, 1)
    if by_heads:
        query_places, segment_query = all_places, segment_whole
        cosine_back, sine_back = cosine_all[:, None], sine_all[:, None]
    else:
        query_places, segment_query = own_start + jnp.arange(group_len), segment_ids
        cosine_back, sine_back = cosine[:, None], sine_table[:, None]
    allowed = (all_places[None, None, :] <= query_places[None, :, None]) & (
        segment_whole[:, None, :] == segment_query[:, :, None]
    )

    def to_heads(values):
        parts = values.shape[2]
        values = values.transpose(3, 2, 0, 1, 4)
        came = lax.all_to_all(values, "seq", 0, 0, tiled=True)
        came = came.reshape(n_seq, HEADS // n_seq, parts, seq_count, group_len, HEAD_DIM)
        came = came.transpose(2, 3, 1, 0, 4, 5)
        return came.reshape(parts, seq_count, HEADS // n_seq, length, HEAD_DIM)

    def to_tokens(values):
        parts = values.shape[0]
        own = HEADS // n_seq
        values = values.reshape(parts, seq_count, own, n_seq, group_len, HEAD_DIM)
        values = values.transpose(3, 2, 0, 1, 4, 5)
        came = lax.all_to_all(values, "seq", 0, 0, tiled=True)
        came = came.reshape(HEADS, parts, seq_count, group_len, HEAD_DIM)
        return came.transpose(1, 2, 3, 0, 4)

    scaling = 1.0 / math.sqrt(HEAD_DIM)

    def attention(queries, keys, values):
        if by_heads:
            queries, keys, values = to_heads(jnp.stack([queries, keys, values], axis=2))
        else:
            queries = queries.transpose(0, 2, 1, 3)
            keys, values = (
                lax.all_gather(item, "seq", axis=1, tiled=True).transpose(0, 2, 1, 3)
                for item in (keys, values)
            )
        scores = jnp.einsum("shqd,shkd->shqk", queries, keys, preferred_element_type=F32)
        scores = jnp.where(allowed[:, None], scores * scaling, -1e30)
        exponent = jnp.exp(scores - jnp.max(scores, axis=-1, keepdims=True))
        soft_full = exponent / jnp.sum(exponent, axis=-1, keepdims=True)
        mixed = jnp.einsum(
            "shqk,shkd->shqd", soft_full.astype(BF16), values, preferred_element_type=F32
        ).astype(BF16)
        if by_heads:
            mixed = to_tokens(mixed[None])[0]
        else:
            mixed = mixed.transpose(0, 2, 1, 3)
        return mixed.reshape(tokens, width), (queries, keys, values, soft_full)

    def attention_back(mixed_grad, saved):
        queries, keys, values, soft_full = saved
        soft_grad = jnp.einsum("shqd,shkd->shqk", mixed_grad, values, preferred_element_type=F32)
        inner_sum = jnp.sum(soft_full * soft_grad, axis=-1, keepdims=True)
        score_grad = (soft_full * (soft_grad - inner_sum)).astype(BF16)
        query_grad = (
            jnp.einsum("shqk,shkd->shqd", score_grad, keys, preferred_element_type=F32) * scaling
        )
        key_grad = (
            jnp.einsum("shqk,shqd->shkd", score_grad, queries, preferred_element_type=F32)
            * scaling
        )
        value_grad = jnp.einsum(
            "shqk,shqd->shkd", soft_full.astype(BF16), mixed_grad, preferred_element_type=F32
        )
        if by_heads:
            query_grad = rotate(query_grad, cosine_back, -sine_back).astype(BF16)
            key_grad = rotate(key_grad, cosine_back, -sine_back).astype(BF16)
            value_grad = value_grad.astype(BF16)
            return jnp.stack([query_grad, key_grad, value_grad])
        key_grad, value_grad = (
            lax.psum_scatter(item.astype(BF16), "seq", scatter_dimension=2, tiled=True).astype(F32)
            for item in (key_grad, value_grad)
        )
        query_grad = rotate(query_grad, cosine_back, -sine_back).astype(BF16)
        key_grad = rotate(key_grad, cosine_back, -sine_back).astype(BF16)
        grads = jnp.stack([query_grad, key_grad, value_grad.astype(BF16)])
        return grads.transpose(0, 1, 3, 2, 4)

    embed_flat = embedding.reshape(tokens, width)
    embed_part = product(embed_flat, adapt_full[width:])
    root_stack = jnp.concatenate(
        [
            right_root_adapt.astype(BF16)[:, None],
            right_root_attn.astype(BF16).transpose(1, 0, 2),
            right_root_down.astype(BF16)[:, None],
            left_root_gateup.astype(BF16).transpose(1, 0, 2),
        ],
        axis=1,
    )
    root_stack = root_stack.reshape(root_stack.shape[0], 8 * width)
    roots = []

    def forward(latent_low):
        start_sum = product(latent_low, adapt_full[:width]) + embed_part
        scale_one = norm_scale(start_sum)
        normed_one = (start_sum * scale_one * gain_values[0]).astype(BF16)
        head_shape = (seq_count, group_len, HEADS, HEAD_DIM)
        turn_cos, turn_sin = cosine[:, :, None, :], sine_table[:, :, None, :]
        queries = product(normed_one, query_full).reshape(head_shape)
        queries = rotate(queries, turn_cos, turn_sin).astype(BF16)
        keys = product(normed_one, key_full).reshape(head_shape)
        keys = rotate(keys, turn_cos, turn_sin).astype(BF16)
        values = product(normed_one, value_full).astype(BF16).reshape(head_shape)
        tied = len(roots) > 0
        if not tied:
            tied_stack, queries = tie(root_stack, queries)
            roots.append(lax.all_gather(tied_stack, AXES, axis=0, tiled=True))
        mixed_heads, attended = attention(queries, keys, values)
        if tied:
            roots[0], mixed_heads = tie(roots[0], mixed_heads)
        branch = product(mixed_heads, out_full)
        scale_two = norm_scale(branch)
        middle = start_sum + branch * scale_two * gain_values[1]
        scale_three = norm_scale(middle)
        normed_three = (middle * scale_three * gain_values[2]).astype(BF16)
        both = product(normed_three, gateup_full)
        gate_value, upward = both[:, :hidden_width], both[:, hidden_width:]
        hidden = (jax.nn.silu(gate_value) * upward).astype(BF16)
        feed_out = product(hidden, down_full)
        scale_four = norm_scale(feed_out)
        result = middle + feed_out * scale_four * gain_values[3]
        saved_values = (
            start_sum,
            scale_one,
            normed_one,
            attended,
            mixed_heads,
            branch,
            scale_two,
            middle,
            scale_three,
            normed_three,
            gate_value,
            upward,
            hidden,
            feed_out,
            scale_four,
        )
        return (result, saved_values)

    latent_low = latent.reshape(tokens, width)
    latent_state, unused_saved = forward(latent_low)
    latent_low = latent_state.astype(BF16)
    final_state, saved_values = forward(latent_low)
    (
        start_sum,
        scale_one,
        normed_one,
        attended,
        mixed_heads,
        branch,
        scale_two,
        middle,
        scale_three,
        normed_three,
        gate_value,
        upward,
        hidden,
        feed_out,
        scale_four,
    ) = saved_values
    factor = 1.0 / math.sqrt(seq_count * n_dp * length)
    incoming = cotangent.astype(F32).reshape(tokens, width)
    feed_grad, gain_four = norm_back(feed_out, scale_four, gain_values[3], incoming)
    feed_grad = feed_grad.astype(BF16)
    down_sum = Reduction(links, width)
    hidden_pair = down_sum.early(hidden)
    normed_three_pair = down_sum.early(normed_three)
    mixed_pair = down_sum.early(mixed_heads)
    normed_one_pair = down_sum.early(normed_one)
    joined_pair = down_sum.early(jnp.concatenate([latent_low, embed_flat], axis=1))
    down_sum.send(hidden_pair, feed_grad)
    hidden_grad = against(feed_grad, down_full)
    gate_grad = (hidden_grad * upward * silu_grad(gate_value)).astype(BF16)
    up_grad = (hidden_grad * jax.nn.silu(gate_value)).astype(BF16)
    gateup_sum = Reduction(links, hidden_width)
    gateup_sum.send(normed_three_pair, gate_grad)
    gateup_sum.send(normed_three_pair, up_grad)
    both_grad = jnp.concatenate([gate_grad, up_grad], axis=1)
    normed_three_grad = against(both_grad, gateup_full)
    middle_grad, gain_three = norm_back(middle, scale_three, gain_values[2], normed_three_grad)
    middle_grad = middle_grad + incoming
    branch_grad, gain_two = norm_back(branch, scale_two, gain_values[1], middle_grad)
    branch_grad = branch_grad.astype(BF16)
    mixed_grad = against(branch_grad, out_full).astype(BF16)
    rest_sum = Reduction(links, width)
    rest_sum.send(mixed_pair, branch_grad)
    down_sum.add()
    (mixed_grad,) = tick([down_sum], mixed_grad)
    mixed_grad = mixed_grad.reshape(seq_count, group_len, HEADS, HEAD_DIM)
    if by_heads:
        mixed_grad = to_heads(mixed_grad[:, :, None])[0]
    else:
        mixed_grad = mixed_grad.transpose(0, 2, 1, 3)
    down_sum.cross(0)
    gateup_sum.add()
    gateup_sum.cross(0)
    (mixed_grad,) = tick([down_sum], mixed_grad)
    grads = attention_back(mixed_grad, attended)
    for step in cross_steps[1:]:
        down_sum.cross(step)
        gateup_sum.cross(step)
    if by_heads:
        grads = to_tokens(grads)
    query_pre, key_pre, value_pre = grads.reshape(3, tokens, width)
    query_pre, key_pre, value_pre = tick([down_sum], query_pre, key_pre, value_pre)
    rest_sum.send(normed_one_pair, jnp.concatenate([query_pre, key_pre, value_pre], axis=1))
    normed_one_grad = (
        against(query_pre, query_full) + against(key_pre, key_full) + against(value_pre, value_full)
    )
    start_grad, gain_one = norm_back(start_sum, scale_one, gain_values[0], normed_one_grad)
    start_grad = (start_grad + middle_grad).astype(BF16)
    rest_sum.send(joined_pair, start_grad)
    gain_sums = jnp.stack([gain_one, gain_two, gain_three, gain_four])
    gain_sums = gain_sums.reshape(4, links.count, gain_share).transpose(1, 0, 2)
    gain_sums = gain_sums.reshape(links.count, 1, 4 * gain_share)
    gain_sums = jnp.pad(gain_sums, ((0, 0), (0, 7), (0, width - 4 * gain_share)))
    rest_sum.send_rows(gain_sums.reshape(-1, width))
    rest_sum.add()
    root_rows = roots[0]
    (start_grad,) = tick([down_sum, rest_sum], start_grad)
    rest_sum.cross(0)
    for step in inner_steps:
        gateup_sum.inside(step)
    tick([rest_sum, gateup_sum])
    gate_shards = (gateup_sum.parts[0] * factor).reshape(2, -1, hidden_width)
    gate_low = jnp.concatenate([gate_shards[0], gate_shards[1]], axis=1).astype(BF16)
    for step in cross_steps[1:]:
        rest_sum.cross(step)
    for step in inner_steps:
        down_sum.inside(step)
    tick([rest_sum, down_sum])
    reduced_down = down_sum.parts[0] * factor
    first = Gathering(links, [reduced_down.astype(BF16)])
    left_root_adapt, left_root_attn, left_root_down, right_root_gateup, reduced_down = tie(
        left_root_adapt, left_root_attn, left_root_down, right_root_gateup, reduced_down
    )
    rest_sum.inside(0)
    first.inside(0)
    tick([rest_sum, first])
    for step in inner_steps[1:]:
        rest_sum.inside(step)
        first.inside(step)
    (gate_low,) = tick([rest_sum, first], gate_low)
    full_both = lax.all_gather(gate_low, AXES, axis=0, tiled=True)
    reduced_rest = rest_sum.parts[0] * factor
    row_share = width // links.count
    attn_shards = reduced_rest[: 4 * row_share].reshape(4, row_share, width)
    attn_shards = jnp.concatenate([attn_shards[1:], attn_shards[:1]], axis=0)
    reduced_adapt = reduced_rest[4 * row_share : 6 * row_share]
    reduced_gains = reduced_rest[6 * row_share, : 4 * gain_share].reshape(4, gain_share)
    third = Gathering(
        links, [attn_shards[i].astype(BF16) for i in range(4)] + [reduced_adapt.astype(BF16)]
    )
    third.inside(0)
    first.cross(0)
    tick([third, first])
    def statistics(shard, whole, left_stat, right_stat, left_root):
        rows, columns = whole.shape
        new_left = 0.5 * left_stat + (0.5 / columns) * against(shard.astype(BF16), whole)
        count = right_stat.shape[0]
        own = lax.dynamic_slice_in_dim(whole, links.index * count, count, 1).T
        if left_root is None:
            return (new_left, 0.5 * right_stat + (0.5 / rows) * product(own, whole), None)
        own_count = left_root.shape[0]
        both = product(jnp.concatenate([left_root.astype(BF16), own], axis=0), whole)
        return (new_left, 0.5 * right_stat + (0.5 / rows) * both[own_count:], both[:own_count])

    def whole_step(part, which, rows):
        root = root_rows[:, which * width : (which + 1) * width]
        return product(part.astype(BF16), root) * (1.0 / math.sqrt(rows))

    for step in inner_steps[1:]:
        third.inside(step)
    for step in cross_steps[1:]:
        first.cross(step)
    tick([third, first])
    first.core()
    fits = row_share % 16 == 0
    third.cross(0)
    tick([third, first])
    for step in cross_steps[1:]:
        third.cross(step)
    if fits:
        down_group = (
            first.sources(),
            reduced_down[None],
            left_down[None],
            right_down[None],
            left_root_down[None],
            weight_down[None],
            [5],
        )
        ((new_left_down, new_right_down, new_down),) = shampoo(links, [down_group], root_rows)
        new_left_down, new_right_down, new_down = new_left_down[0], new_right_down[0], new_down[0]
    else:
        (full_down,) = first.finish()
        new_left_down, new_right_down, down_part = statistics(
            reduced_down, full_down, left_down, right_down, left_root_down
        )
        new_down = weight_down - whole_step(down_part, 5, hidden_width)
    full_both, new_down = tie(full_both, new_down)
    if fits:
        sources = [Source([full_both], i * hidden_width, width, hidden_width) for i in range(2)]
        ((new_left_gateup, new_right_gateup, step_columns),) = shampoo(
            links,
            [
                (
                    sources,
                    gate_shards,
                    left_gateup,
                    right_gateup,
                    right_root_gateup,
                    None,
                    [6, 7],
                )
            ],
            root_rows,
        )
        step_columns = step_columns.transpose(0, 2, 1)
    else:
        whole_gates = [full_both[:, :hidden_width], full_both[:, hidden_width:]]
        gateup_parts = [
            statistics(gate_shards[i], whole_gates[i], left_gateup[i], right_gateup[i], None)
            for i in range(2)
        ]
        step_columns = []
        for i in range(2):
            turned = against(whole_gates[i], right_root_gateup[i].astype(BF16)).astype(BF16)
            root = root_rows[:, (6 + i) * width : (7 + i) * width]
            step_columns.append(product(root, turned).astype(BF16))
        step_columns = jnp.stack(step_columns)
        new_left_gateup = jnp.stack([member[0] for member in gateup_parts])
        new_right_gateup = jnp.stack([member[1] for member in gateup_parts])
    ff_share = step_columns.shape[2]
    step_columns = step_columns.reshape(2, links.count, row_share, ff_share).transpose(1, 0, 2, 3)
    new_down, step_columns = tick([third], new_down, step_columns)
    third.core()
    tick([third])
    step_rows = lax.all_to_all(step_columns, AXES, 0, 0, tiled=True)

    grad_embedding = against(start_grad, adapt_full[width:]).reshape(
        seq_count, group_len, width
    )
    if fits:
        sources = third.sources()
        attn_group = (
            sources[:4],
            attn_shards,
            left_attn,
            right_attn,
            left_root_attn,
            weight_attn,
            [1, 2, 3, 4],
        )
        adapt_group = (
            sources[4:],
            reduced_adapt[None],
            left_adapt[None],
            right_adapt[None],
            left_root_adapt[None],
            weight_adapt[None],
            [0],
        )
        (
            (new_left_attn, new_right_attn, new_attn),
            (new_left_adapt, new_right_adapt, new_adapt),
        ) = shampoo(links, [attn_group, adapt_group], root_rows)
        new_left_adapt, new_right_adapt, new_adapt = (
            new_left_adapt[0],
            new_right_adapt[0],
            new_adapt[0],
        )
    else:
        *attn_wholes, full_adapt = third.finish()
        attn_parts = [
            statistics(
                attn_shards[i], attn_wholes[i], left_attn[i], right_attn[i], left_root_attn[i]
            )
            for i in range(4)
        ]
        new_attn = weight_attn - jnp.stack(
            [whole_step(attn_parts[i][2], 1 + i, width) for i in range(4)]
        )
        new_left_attn = jnp.stack([member[0] for member in attn_parts])
        new_right_attn = jnp.stack([member[1] for member in attn_parts])
        new_left_adapt, new_right_adapt, adapt_part = statistics(
            reduced_adapt, full_adapt, left_adapt, right_adapt, left_root_adapt
        )
        new_adapt = weight_adapt - whole_step(adapt_part, 0, 2 * width)
    step_rows, new_adapt = tie(step_rows, new_adapt)
    step_gateup = step_rows.transpose(1, 2, 0, 3).reshape(2, row_share, hidden_width)
    new_gateup = weight_gateup - step_gateup.astype(F32) * (1.0 / math.sqrt(width))
    new_gain_moment = 0.5 * gain_moment + 0.5 * reduced_gains * reduced_gains
    new_norm_gains = norm_gains - 0.5 * reduced_gains / (jnp.sqrt(new_gain_moment) + 1e-08)
    latent_out = final_state.reshape(seq_count, group_len, width).astype(BF16)
    return (
        latent_out,
        grad_embedding,
        reduced_adapt,
        attn_shards,
        gate_shards,
        reduced_down,
        reduced_gains,
        new_left_adapt,
        new_right_adapt,
        new_left_attn,
        new_right_attn,
        new_left_gateup,
        new_right_gateup,
        new_left_down,
        new_right_down,
        new_adapt,
        new_attn,
        new_gateup,
        new_down,
        new_gain_moment,
        new_norm_gains,
    )

def solution(mesh):
    return jax.shard_map(
        body,
        mesh=mesh,
        in_specs=(
            P("dp", "seq", None),
            P("dp", "seq", None),
            P("dp", "seq"),
            P("dp", "seq", None),
            P(("dp", "seq"), None),
            P(None, ("dp", "seq"), None),
            P(None, ("dp", "seq"), None),
            P(("dp", "seq"), None),
            P(None, ("dp", "seq")),
            P(("dp", "seq"), None),
            P(("dp", "seq"), None),
            P(None, ("dp", "seq"), None),
            P(None, ("dp", "seq"), None),
            P(None, ("dp", "seq"), None),
            P(None, ("dp", "seq"), None),
            P(("dp", "seq"), None),
            P(("dp", "seq"), None),
            P(("dp", "seq"), None),
            P(("dp", "seq"), None),
            P(None, ("dp", "seq"), None),
            P(None, ("dp", "seq"), None),
            P(None, ("dp", "seq"), None),
            P(None, ("dp", "seq"), None),
            P(("dp", "seq"), None),
            P(("dp", "seq"), None),
            P(None, ("dp", "seq")),
        ),
        out_specs=(
            P("dp", "seq", None),
            P("dp", "seq", None),
            P(("dp", "seq"), None),
            P(None, ("dp", "seq"), None),
            P(None, ("dp", "seq"), None),
            P(("dp", "seq"), None),
            P(None, ("dp", "seq")),
            P(("dp", "seq"), None),
            P(("dp", "seq"), None),
            P(None, ("dp", "seq"), None),
            P(None, ("dp", "seq"), None),
            P(None, ("dp", "seq"), None),
            P(None, ("dp", "seq"), None),
            P(("dp", "seq"), None),
            P(("dp", "seq"), None),
            P(("dp", "seq"), None),
            P(None, ("dp", "seq"), None),
            P(None, ("dp", "seq"), None),
            P(("dp", "seq"), None),
            P(None, ("dp", "seq")),
            P(None, ("dp", "seq")),
        ),
        check_vma=False,
    )
```
